256 devices in a mesh: replica: 16 (over x_hi, y, core), tensor: 16 (over z, x_lo).
Axes of the slice: x: 4 (x_hi: 2, x_lo: 2; x = x_hi * 2 + x_lo), y: 4, z: 8, core: 2. Of those that a mesh axis runs over, the one named last changes fastest.
Arguments:
- hidden: bfloat16 [2, 16, 4, 8192], P(None, 'replica', None, 'tensor'), may hold values from -12 to 12
- resident: bfloat16 [2, 8192, 2048], P(None, 'tensor'), may hold values from -6 to 6
- delta_codes: bfloat16 [2, 8192, 2048], P(None, 'tensor', 'replica'), may hold values from -4 to 4
- scales: bfloat16 [2, 8192, 16], P(None, 'tensor', 'replica'), may hold values from 0.049804688 to 0.5
- owner_map: int32 [16], replicated, may hold values from 0 to 15, each once
- key_value_bias: bfloat16 [2, 2048], replicated, may hold values from -6 to 6
- queries: bfloat16 [2, 16, 4, 64, 128], P(None, 'replica'), may hold values from -110 to 110
- key_cache: bfloat16 [2, 16, 8192, 8, 128], P(None, 'replica', 'tensor'), may hold values from -5 to 5
- value_cache: bfloat16 [2, 16, 8192, 8, 128], P(None, 'replica', 'tensor'), may hold values from -5 to 5
- lengths: int32 [16], P('replica'), may hold values from 1024 to 8188, as said below
Outputs:
- updated_weights: bfloat16 [2, 8192, 2048], P(None, 'tensor')
- attention_out: bfloat16 [2, 16, 4, 64, 128], P(None, 'replica', None, 'tensor')
The draws below stay inside these ranges and needn't reach their ends.
Inputs may be any that keep to these rules, and one draw needn't show every extreme that they name: owner_map is a permutation of 0 to 15. `lengths`: sequence 0 has exactly 8188 filled slots.
All inputs are finite; a program needn't handle non-finite values.
Results may differ from the reference program's by a relative error of at most 0.008.
Values may be sent and summed in bfloat16 or wider, within the bound.
A program may use at most 128 MiB of HBM per device.

```python
import math
import jax
import jax.numpy as jnp
from jax import lax

D = 8192
QH = 64
KVH = 8
HD = 128
LAYERS = 2
STEPS = 4
CACHE = 8192
KVW = 2048
SEQS = 16
N_REPLICA = 16


def draw_key_cache(key, part):
    key = jax.random.fold_in(key, 1)
    base = jnp.clip(jax.random.normal(key, (LAYERS, SEQS, CACHE, KVH, HD), jnp.float32), -4.5, 4.5)
    return base.astype(jnp.bfloat16)


def draw_queries(key, part):
    key = jax.random.fold_in(key, 2)
    base = 2.0 * jnp.clip(jax.random.normal(key, (LAYERS, SEQS, STEPS, QH, HD), jnp.float32), -5.0, 5.0)
    return base.astype(jnp.bfloat16)


def draw_lengths(key, part):
    key = jax.random.fold_in(key, 3)
    drawn = jax.random.randint(key, (SEQS,), CACHE // 8, CACHE - STEPS + 1).astype(jnp.int32)
    return drawn.at[0].set(CACHE - STEPS)


def level_of(rng, shape, pieces, low, largest):
    loudness = 1.0
    for dim, parts in pieces:
        steps = jax.random.uniform(jax.random.fold_in(jax.random.fold_in(rng, 6), dim), (parts,), jnp.float32, low / len(pieces), largest / len(pieces))
        loudness = loudness * jnp.repeat(jnp.exp(steps), shape[dim] // parts).reshape((-1,) + (1,) * (len(shape) - 1 - dim))
    return loudness


def gaussian(own_key, extent, spread, most, split=(), dtype=jnp.bfloat16):
    level = level_of(own_key, extent, split, -0.22, 0.18) if split else 1.0
    values = jax.random.normal(own_key, extent, jnp.float32) * spread * level
    return jnp.minimum(jnp.maximum(values, -most), most).astype(dtype)


def setup_inputs(seed: int = 0) -> dict:
    key_of = jax.random.split(jax.random.key(seed), 11)
    return {
        "hidden": gaussian(key_of[0], (LAYERS, SEQS, STEPS, D), 2.0, 12.0, ((1, 16), (3, 16))),
        "resident": gaussian(key_of[1], (LAYERS, D, KVW), 1.0, 6.0, ((1, 16),)),
        "delta_codes": gaussian(key_of[2], (LAYERS, D, KVW), 1.0, 4.0, ((1, 16), (2, 16))),
        "scales": jnp.clip(jnp.exp(math.log(0.5) - 2.306499 * jax.random.uniform(key_of[3], (LAYERS, D, KVW // HD), jnp.float32) ** level_of(key_of[3], (LAYERS, D, KVW // HD), ((1, 16), (2, 16)), -0.2, 0.2)), 0.049804688, 0.5).astype(jnp.bfloat16),
        "owner_map": jax.random.permutation(key_of[4], N_REPLICA).astype(jnp.int32),
        "key_value_bias": gaussian(key_of[5], (LAYERS, KVW), 2.0, 6.0),
        "queries": draw_queries(jax.random.fold_in(key_of[10], 71), 0),
        "key_cache": draw_key_cache(jax.random.fold_in(key_of[10], 71), 0),
        "value_cache": gaussian(key_of[8], (LAYERS, SEQS, CACHE, KVH, HD), 1.0, 5.0, ((1, 16), (2, 16))),
        "lengths": draw_lengths(jax.random.fold_in(key_of[10], 71), 0),
    }


ROPE_BASE = 1000000.0


def rotate(values, positions, is_key):
    half = values.shape[-1] // 2
    index_range = jnp.arange(half).astype(jnp.float32)
    inverse = ROPE_BASE ** (-2.0 * index_range / values.shape[-1])
    angle = positions[:, None] * inverse[None, :]
    cosine = jnp.cos(angle)[:, None, :]
    sine = jnp.sin(angle)[:, None, :]
    former = values[..., :half]
    latter = values[..., half:]
    turned = jnp.concatenate([former * cosine - latter * sine, latter * cosine + former * sine], axis=-1)
    return jnp.where(is_key[None, :, None], turned, values)


def attend(operands):
    query, cached_keys, cached_values, new_keys, new_values, length = operands
    group_size = QH // KVH
    score_scale = HD ** -0.5
    query_f = query.astype(jnp.float32).reshape(STEPS, KVH, group_size, HD)
    scores = jnp.einsum('sghd,pgd->sghp', query_f, cached_keys.astype(jnp.float32)) * score_scale
    inside = jnp.arange(CACHE) < length
    scores = jnp.where(inside[None, None, None, :], scores, -jnp.inf)
    fresh_scores = jnp.einsum('sghd,jgd->sghj', query_f, new_keys.astype(jnp.float32)) * score_scale
    causal = jnp.arange(STEPS)[None, :] <= jnp.arange(STEPS)[:, None]
    fresh_scores = jnp.where(causal[:, None, None, :], fresh_scores, -jnp.inf)
    highest = jnp.maximum(jnp.max(scores, axis=-1), jnp.max(fresh_scores, axis=-1))
    expo = jnp.exp(scores - highest[..., None])
    fresh_expo = jnp.exp(fresh_scores - highest[..., None])
    denominator = jnp.sum(expo, axis=-1) + jnp.sum(fresh_expo, axis=-1)
    weights = lax.optimization_barrier(expo.astype(jnp.bfloat16)).astype(jnp.float32)
    fresh_weights = lax.optimization_barrier(fresh_expo.astype(jnp.bfloat16)).astype(jnp.float32)
    summed = jnp.einsum('sghp,pgd->sghd', weights, cached_values.astype(jnp.float32))
    summed = summed + jnp.einsum('sghj,jgd->sghd', fresh_weights, new_values.astype(jnp.float32))
    result = summed / denominator[..., None]
    return result.reshape(STEPS, QH, HD).astype(jnp.bfloat16)


def reference(hidden, resident, delta_codes, scales, owner_map, key_value_bias, queries, key_cache, value_cache, lengths):
    group_cols = KVW // N_REPLICA
    group_blocks = (KVW // HD) // N_REPLICA
    width_scale = D ** -0.5
    positions = (lengths[:, None] + jnp.arange(STEPS).astype(jnp.int32)[None, :]).reshape(-1).astype(jnp.float32)
    is_key = jnp.arange(2 * KVH) % 2 == 0
    weight_list = []
    output_list = []
    for layer_index in range(LAYERS):
        slot_codes = delta_codes[layer_index].reshape(D, N_REPLICA, group_cols)[:, owner_map, :].reshape(D, KVW)
        slot_scales = scales[layer_index].reshape(D, N_REPLICA, group_blocks)[:, owner_map, :].reshape(D, KVW // HD)
        delta_full = slot_codes.astype(jnp.float32).reshape(D, KVW // HD, HD) * slot_scales.astype(jnp.float32)[:, :, None]
        new_weights = (resident[layer_index].astype(jnp.float32) + delta_full.reshape(D, KVW)).astype(jnp.bfloat16)
        token_rows = hidden[layer_index].reshape(SEQS * STEPS, D)
        projected = jnp.dot(token_rows, new_weights, preferred_element_type=jnp.float32) * width_scale
        projected = projected + key_value_bias[layer_index].astype(jnp.float32)[None, :]
        key_values = rotate(projected.reshape(SEQS * STEPS, 2 * KVH, HD), positions, is_key)
        key_values = key_values.astype(jnp.bfloat16).reshape(SEQS, STEPS, KVH, 2, HD)
        outputs = lax.map(attend, (queries[layer_index], key_cache[layer_index], value_cache[layer_index],
                                   key_values[:, :, :, 0, :], key_values[:, :, :, 1, :], lengths))
        weight_list.append(new_weights)
        output_list.append(outputs)
    return jnp.stack(weight_list), jnp.stack(output_list)
```

```python
import functools
import math

import jax
import jax.numpy as jnp
import numpy as np
from jax import lax
from jax.experimental import pallas as pl
from jax.experimental.pallas import tpu as pltpu
from jax.sharding import PartitionSpec as P

MESH = pl.DeviceIdType.MESH
ROPE_BASE = 1000000.0
MIB = 1 << 20
NEG = -1e30

LAYERS = 2
STEPS = 4
ROWS = 512
HD = 128
SLOTS = 16
PEERS = 16
HEADS = 64
KVH = 8
QROWS = STEPS * HEADS
OWN = QROWS // PEERS
SPOTS = 512
COLS = SPOTS * KVH
WIDE = 512
CHUNKS = 4
HALF = ROWS * LAYERS // CHUNKS
EXP_SCALE = HD**-0.5 * math.log2(math.e)


def place():
    replica = lax.axis_index("replica")
    return replica // 8, (replica // 2) % 4, replica % 2, lax.axis_index("tensor")


def slot_of(xh, y, c):
    return (xh * 4 + y) * 2 + c


def gather_kernel(
    map_hbm, len_ref, hid_hbm, res_hbm, code_hbm, scale_hbm, bias_hbm, inv_hbm, q_hbm, k_hbm, v_hbm,
    gat, out_ref,
    map_ref, hid_ref, res, code_ref, scale_ref, bias_ref, inv_ref, q_ref, kbuf, vbuf, qp, sbuf, top, total, acc, asend, arecv, proj, psend, precv,
    load_sem, r_sem, own_sem, y2_sem, cross_sem, far_sem, sib_sem,
    as_sem, ar_sem, ps_sem, pr_sem,
):
    xh, y, c, t = place()
    me = slot_of(xh, y, c)

    pairs = [
        (map_hbm, map_ref), (scale_hbm, scale_ref), (code_hbm, code_ref), (res_hbm, res),
        (q_hbm, q_ref), (k_hbm, kbuf), (v_hbm, vbuf),
        (hid_hbm, hid_ref), (bias_hbm, bias_ref), (inv_hbm, inv_ref),
    ]
    loads = [pltpu.make_async_copy(a, b, load_sem.at[i]) for i, (a, b) in enumerate(pairs)]
    for load in loads:
        load.start()

    def device(x2, y2, c2):
        return (slot_of(x2, y2, c2), t)

    y_up, y_down = (y + 1) % 4, (y + 3) % 4
    y_far = (y + 2) % 4
    to_up, to_down = device(xh, y_up, c), device(xh, y_down, c)
    to_x, to_sib = device(1 - xh, y, c), device(xh, y, 1 - c)

    barrier = pltpu.get_barrier_semaphore()
    for partner in (to_up, to_down, to_x, to_sib):
        pl.semaphore_signal(barrier, inc=1, device_id=partner, device_id_type=MESH)

    def greet(k, carry):
        pl.semaphore_signal(barrier, inc=1, device_id=(me, (t + k) % PEERS), device_id_type=MESH)
        return carry

    lax.fori_loop(1, PEERS, greet, 0)

    loads[0].wait()
    group = jnp.int32(0)
    for g in range(SLOTS):
        group = group + jnp.where(map_ref[g] == me, g, 0)
    for load in loads[1:4]:
        load.wait()
    group_all = jnp.broadcast_to(group.astype(jnp.float32), (HD, HD)).astype(jnp.bfloat16)
    for layer in range(LAYERS):
        for part in range(ROWS // HD):
            rows = pl.ds(part * HD, HD)
            line = scale_ref[pl.ds(layer, 1), rows].astype(jnp.float32)
            column = jnp.transpose(jnp.broadcast_to(line, (HD, HD)))
            code = code_ref[layer, rows, :].astype(jnp.float32)
            base = res[layer, rows, :HD]
            for g in range(1, SLOTS):
                base = jnp.where(group_all == g, res[layer, rows, g * HD : (g + 1) * HD], base)
            base = base.astype(jnp.float32)
            gat[me, layer, rows, :] = (base + code * column).astype(jnp.bfloat16)

    pl.semaphore_wait(barrier, PEERS - 1 + 4)

    def piece(slot, j):
        return gat.at[slot, j // 2, pl.ds(pl.multiple_of((j % 2) * HALF, HALF), HALF), :]

    def send(slot, j, sem, target):
        return pltpu.make_async_remote_copy(
            src_ref=piece(slot, j), dst_ref=piece(slot, j), send_sem=sem,
            recv_sem=r_sem.at[slot, j], device_id=target, device_id_type=MESH,
        )

    def arrived(slot, j):
        send(slot, j, r_sem.at[slot, j], to_sib).wait_recv()

    def loop(low, high, body):
        def step(j, carry):
            body(j)
            return carry

        lax.fori_loop(low, high, step, 0)

    s_up, s_down = slot_of(xh, y_up, c), slot_of(xh, y_down, c)
    s_far, s_x = slot_of(xh, y_far, c), slot_of(1 - xh, y, c)
    x_up, x_down = slot_of(1 - xh, y_up, c), slot_of(1 - xh, y_down, c)
    x_far = slot_of(1 - xh, y_far, c)

    def own_copies(j):
        return [
            send(me, j, own_sem.at[0, j], to_up),
            send(me, j, own_sem.at[1, j], to_down),
            send(me, j, own_sem.at[2, j], to_x),
            send(me, j, own_sem.at[3, j], to_sib),
        ]

    def onward(j):
        up = 1 - 2 * (j % 2)
        return slot_of(xh, (y + 4 - up) % 4, c), device(xh, (y + 4 + up) % 4, c)

    def y2_copy(j):
        slot, target = onward(j)
        return send(slot, j, y2_sem.at[j], target)

    def cross_copies(j):
        return [send(s_x, j, cross_sem.at[0, j], to_up), send(s_x, j, cross_sem.at[1, j], to_down)]

    def far_copy(j):
        return send(s_far, j, far_sem.at[j], to_x)

    sib_slots = [s_up, s_down, s_x, s_far, x_up, x_down, x_far]

    def sib_copy(i, j):
        return send(sib_slots[i], j, sib_sem.at[i, j], to_sib)

    def own_step(j):
        for copy in own_copies(j):
            copy.start()

    loop(0, CHUNKS, own_step)

    for load in loads[4:5]:
        load.wait()
    row = lax.broadcasted_iota(jnp.int32, (QROWS, QROWS), 0)
    col = lax.broadcasted_iota(jnp.int32, (QROWS, QROWS), 1)
    source = ((row // STEPS) % STEPS) * HEADS + (row // OWN) * STEPS + row % STEPS
    pick = jnp.where(col == source, 1.0, 0.0).astype(jnp.bfloat16)
    for layer in range(LAYERS):
        qp[layer] = jnp.dot(pick, q_ref[layer], preferred_element_type=jnp.float32).astype(
            jnp.bfloat16
        )
    length = len_ref[0]
    limit = (length - t * SPOTS) * KVH
    lanes = lax.broadcasted_iota(jnp.int32, (1, WIDE), 1)
    lane = lax.broadcasted_iota(jnp.int32, (QROWS, HD), 1)

    def scores(layer):
        top[...] = jnp.full((QROWS, HD), NEG, jnp.float32)

        def body(n):
            first = pl.multiple_of(n * WIDE, WIDE)
            s = lax.dot_general(
                qp[layer], kbuf[layer, pl.ds(first, WIDE), :], (((1,), (1,)), ((), ())),
                preferred_element_type=jnp.float32,
            )
            within = lanes + first < limit
            for g in range(KVH):
                rows = slice(g * 32, g * 32 + 32)
                bias = jnp.where(within & (lanes % KVH == g), 0.0, NEG)
                s_g = s[rows] + bias
                sbuf[rows, pl.ds(first, WIDE)] = s_g
                high = top[rows]
                for i in range(WIDE // HD):
                    high = jnp.maximum(high, s_g[:, i * HD : (i + 1) * HD])
                top[rows] = high

        loop(0, COLS // WIDE, body)
        top[...] = jnp.broadcast_to(jnp.max(top[...], axis=1, keepdims=True), (QROWS, HD))

    def values(layer):
        total[...] = jnp.zeros((QROWS, HD), jnp.float32)
        acc[...] = jnp.zeros((QROWS, HD), jnp.float32)

        def body(n):
            first = pl.multiple_of(n * WIDE, WIDE)
            high = top[...]
            added = total[...]
            parts = []
            for i in range(WIDE // HD):
                e = jnp.exp2((sbuf[:, pl.ds(first + i * HD, HD)] - high) * EXP_SCALE)
                added = added + e
                parts.append(e.astype(jnp.bfloat16))
            total[...] = added
            weights = jnp.concatenate(parts, axis=1)
            acc[...] += jnp.dot(
                weights, vbuf[layer, pl.ds(first, WIDE), :], preferred_element_type=jnp.float32
            )

        loop(0, COLS // WIDE, body)
        asend[:, layer * OWN : (layer + 1) * OWN, :] = acc[...].reshape(PEERS, OWN, HD)
        whole = jnp.sum(total[...], axis=1, keepdims=True)
        before = asend[:, 2 * OWN :, :].reshape(QROWS, HD) if layer else jnp.zeros((QROWS, HD))
        kept = jnp.where(lane == 2 * layer, top[...], before)
        kept = jnp.where(lane == 2 * layer + 1, jnp.broadcast_to(whole, (QROWS, HD)), kept)
        asend[:, 2 * OWN :, :] = kept.reshape(PEERS, OWN, HD)

    def near_step(j):
        slot, _ = onward(j)
        other = slot_of(xh, (y + 4 + 1 - 2 * (j % 2)) % 4, c)
        arrived(slot, j)
        y2_copy(j).start()
        arrived(s_x, j)
        for copy in cross_copies(j):
            copy.start()
        arrived(other, j)
        for i in range(3):
            sib_copy(i, j).start()

    loads[5].wait()
    scores(0)
    loads[6].wait()
    values(0)
    loop(0, 2, near_step)
    scores(1)
    values(1)
    loop(2, CHUNKS, near_step)

    def peer_copy(src, dst, s_sem, rr_sem, k):
        target = (t + k) % PEERS
        return pltpu.make_async_remote_copy(
            src_ref=src(target), dst_ref=dst.at[t], send_sem=s_sem.at[target],
            recv_sem=rr_sem.at[t], device_id=(me, target), device_id_type=MESH,
        )

    def peer_arrived(src, dst, s_sem, rr_sem, k):
        other = (t + k) % PEERS
        pltpu.make_async_remote_copy(
            src_ref=src(other), dst_ref=dst.at[other], send_sem=s_sem.at[other],
            recv_sem=rr_sem.at[other], device_id=(me, other), device_id_type=MESH,
        ).wait_recv()

    attention = (lambda target: asend.at[target], arecv, as_sem, ar_sem)
    project = (lambda target: psend.at[target // 2], precv, ps_sem, pr_sem)
    loop(1, PEERS, lambda k: peer_copy(*attention, k).start())
    arecv[t] = asend[t]

    for load in loads[7:]:
        load.wait()
    hidden = [hid_ref[layer, 0] for layer in range(LAYERS)]

    def multiply(slot, layer):
        proj[slot, pl.ds(layer * STEPS, STEPS), :] = jnp.dot(
            hidden[layer], gat[slot, layer], preferred_element_type=jnp.float32
        )

    def far_step(j):
        arrived(s_far, j)
        far_copy(j).start()
        sib_copy(3, j).start()

    def settle(slots, layer):
        for slot in slots:
            multiply(slot, layer)

    def flip(slot):
        return slot + 1 - 2 * c

    near = [s_up, s_down, s_x]
    loop(0, 2, far_step)
    for slot in [me]:
        for layer in range(LAYERS):
            multiply(slot, layer)
    for slot in [me] + near:
        loop(0, CHUNKS, lambda j, slot=slot: arrived(flip(slot), j))
    for layer in range(LAYERS):
        settle(near, layer)
        settle([flip(slot) for slot in [me] + near], layer)
    loop(2, CHUNKS, far_step)

    def late_step(j):
        arrived(x_up, j)
        sib_copy(4, j).start()
        arrived(x_down, j)
        sib_copy(5, j).start()
        arrived(x_far, j)
        sib_copy(6, j).start()

    loop(0, 2, late_step)

    loop(1, PEERS, lambda k: peer_arrived(*attention, k))
    joined = []
    for layer in range(LAYERS):
        highs = [arecv[p, 2 * OWN :, 2 * layer : 2 * layer + 1] for p in range(PEERS)]
        high = functools.reduce(jnp.maximum, highs)
        whole = jnp.zeros((OWN, 1), jnp.float32)
        summed = jnp.zeros((OWN, HD), jnp.float32)
        for p in range(PEERS):
            factor = jnp.exp2((highs[p] - high) * EXP_SCALE)
            whole = whole + factor * arecv[p, 2 * OWN :, 2 * layer + 1 : 2 * layer + 2]
            summed = summed + factor * arecv[p, layer * OWN : (layer + 1) * OWN, :]
        joined.append((high, whole, summed))

    turn_row = lax.broadcasted_iota(jnp.int32, (LAYERS * STEPS, HD), 0)
    turn_lane = lax.broadcasted_iota(jnp.int32, (LAYERS * STEPS, HD), 1)
    angle = (length + turn_row % STEPS).astype(jnp.float32) * inv_ref[...]
    cosine = jnp.cos(angle)
    sine = jnp.where(turn_lane < HD // 2, -1.0, 1.0) * jnp.sin(angle)

    far = [s_far, x_up, x_down, x_far]
    for slot in far:
        loop(0, 2, lambda j, slot=slot: arrived(flip(slot), j))
    settle(far + [flip(slot) for slot in far], 0)
    loop(2, CHUNKS, late_step)
    settle(far, 1)
    for slot in far:
        loop(2, CHUNKS, lambda j, slot=slot: arrived(flip(slot), j))
    settle([flip(slot) for slot in far], 1)

    for g in range(SLOTS):
        slot_all = jnp.broadcast_to(map_ref[g], (LAYERS * STEPS, HD))
        line = proj[0]
        for slot in range(1, SLOTS):
            line = jnp.where(slot_all == slot, proj[slot], line)
        psend[g // 2, (g % 2) * 8 : (g % 2) * 8 + 8, :] = line
    loop(1, PEERS, lambda k: peer_copy(*project, k).start())
    precv[t] = psend[t // 2]
    head = t // 2
    bias = bias_ref[:, pl.ds(pl.multiple_of(head * 2 * HD, 2 * HD), 2 * HD)].astype(jnp.float32)
    loop(1, PEERS, lambda k: peer_arrived(*project, k))
    projected = precv[0]
    for p in range(1, PEERS):
        projected = projected + precv[p]
    projected = projected * (ROWS * PEERS) ** -0.5

    def biased(kind):
        part = projected[kind * 8 : kind * 8 + 8]
        line = [
            jnp.broadcast_to(bias[layer : layer + 1, kind * HD : (kind + 1) * HD], (8, HD))
            for layer in range(LAYERS)
        ]
        return part + jnp.where(turn_row < STEPS, line[0], line[1])

    key = biased(0)
    key = (key * cosine + pltpu.roll(key, HD // 2, 1) * sine).astype(jnp.bfloat16)
    value = biased(1).astype(jnp.bfloat16)
    row = lax.broadcasted_iota(jnp.int32, (OWN, LAYERS * STEPS), 0)
    col = lax.broadcasted_iota(jnp.int32, (OWN, LAYERS * STEPS), 1)
    for layer in range(LAYERS):
        query = qp[layer, pl.ds(pl.multiple_of(t * OWN, OWN), OWN), :]
        s = lax.dot_general(
            query, key, (((1,), (1,)), ((), ())), preferred_element_type=jnp.float32
        )
        allowed = (col // STEPS == layer) & (col % STEPS <= row // STEPS)
        s = jnp.where(allowed, s, NEG)
        high, whole, summed = joined[layer]
        top_all = jnp.maximum(high, jnp.max(s, axis=1, keepdims=True))
        e = jnp.exp2((s - top_all) * EXP_SCALE)
        factor = jnp.exp2((high - top_all) * EXP_SCALE)
        whole = whole * factor + jnp.sum(e, axis=1, keepdims=True)
        summed = summed * factor + jnp.dot(
            e.astype(jnp.bfloat16), value, preferred_element_type=jnp.float32
        )
        result = (summed / whole).astype(jnp.bfloat16)
        for step in range(STEPS):
            out_ref[layer, 0, step] = result[step * 4 : step * 4 + 4]

    def sent(j):
        for copy in own_copies(j) + cross_copies(j) + [y2_copy(j), far_copy(j)]:
            copy.wait_send()
        for i in range(len(sib_slots)):
            sib_copy(i, j).wait_send()

    loop(0, CHUNKS, sent)
    loop(1, PEERS, lambda k: peer_copy(*attention, k).wait_send())
    loop(1, PEERS, lambda k: peer_copy(*project, k).wait_send())


def place_kernel(map_ref, gat, part, out_hbm, part_out, sem):
    copies = []
    for group in range(SLOTS):
        for layer in range(LAYERS):
            copy = pltpu.make_async_copy(
                gat.at[map_ref[group], layer],
                out_hbm.at[layer, :, pl.ds(group * HD, HD)],
                sem.at[group, layer],
            )
            copy.start()
            copies.append(copy)
    part_out[...] = part[...]
    for copy in copies:
        copy.wait()


def on_device(
    hidden, resident, delta_codes, scales, owner_map, key_value_bias, queries, key_cache,
    value_cache, lengths,
):
    inverse = (ROPE_BASE ** (-2.0 * np.arange(HD // 2) / HD)).astype(np.float32)
    inverse = jnp.asarray(np.concatenate([inverse, inverse])[None, :])
    smem = pl.BlockSpec(memory_space=pltpu.SMEM)
    vmem = pl.BlockSpec(memory_space=pltpu.VMEM)
    hbm = pl.BlockSpec(memory_space=pltpu.HBM)
    anywhere = pl.BlockSpec(memory_space=pl.ANY)
    dma = pltpu.SemaphoreType.DMA
    f32, bf16 = jnp.float32, jnp.bfloat16
    part_shape = (LAYERS, 1, STEPS, HEADS // PEERS, HD)
    arrays = (
        owner_map, lengths, hidden, resident, delta_codes,
        scales.reshape(LAYERS, ROWS), key_value_bias, inverse,
        queries.reshape(LAYERS, QROWS, HD),
        key_cache.reshape(LAYERS, COLS, HD), value_cache.reshape(LAYERS, COLS, HD),
    )
    gathered, part = pl.pallas_call(
        gather_kernel,
        out_shape=(
            pltpu.VMEM((SLOTS, LAYERS, ROWS, HD), bf16),
            jax.ShapeDtypeStruct(part_shape, bf16),
        ),
        in_specs=[hbm, smem] + [hbm] * 9,
        out_specs=(vmem, vmem),
        scratch_shapes=[
            pltpu.SMEM((SLOTS,), jnp.int32),
            pltpu.VMEM((LAYERS, 1, STEPS, ROWS), bf16),
            pltpu.VMEM((LAYERS, ROWS, SLOTS * HD), bf16),
            pltpu.VMEM((LAYERS, ROWS, HD), bf16),
            pltpu.VMEM((LAYERS, ROWS), bf16),
            pltpu.VMEM((LAYERS, SLOTS * HD), bf16),
            pltpu.VMEM((1, HD), f32),
            pltpu.VMEM((LAYERS, QROWS, HD), bf16),
            pltpu.VMEM((LAYERS, COLS, HD), bf16),
            pltpu.VMEM((LAYERS, COLS, HD), bf16),
            pltpu.VMEM((LAYERS, QROWS, HD), bf16),
            pltpu.VMEM((QROWS, COLS), f32),
            pltpu.VMEM((QROWS, HD), f32),
            pltpu.VMEM((QROWS, HD), f32),
            pltpu.VMEM((QROWS, HD), f32),
            pltpu.VMEM((PEERS, 3 * OWN, HD), f32),
            pltpu.VMEM((PEERS, 3 * OWN, HD), f32),
            pltpu.VMEM((SLOTS, LAYERS * STEPS, HD), f32),
            pltpu.VMEM((PEERS // 2, 16, HD), f32),
            pltpu.VMEM((PEERS, 16, HD), f32),
            dma((10,)),
            dma((SLOTS, CHUNKS)),
            dma((4, CHUNKS)),
            dma((CHUNKS,)),
            dma((2, CHUNKS)),
            dma((CHUNKS,)),
            dma((7, CHUNKS)),
            dma((PEERS,)),
            dma((PEERS,)),
            dma((PEERS,)),
            dma((PEERS,)),
        ],
        compiler_params=pltpu.CompilerParams(
            collective_id=0, has_side_effects=True, vmem_limit_bytes=40 * MIB
        ),
    )(*(a if a.size == 1 else pltpu.with_memory_space_constraint(a, pltpu.HBM) for a in arrays))
    return pl.pallas_call(
        place_kernel,
        out_shape=(
            jax.ShapeDtypeStruct((LAYERS, ROWS, SLOTS * HD), bf16),
            jax.ShapeDtypeStruct(part_shape, bf16),
        ),
        in_specs=[smem, vmem, vmem],
        out_specs=(anywhere, vmem),
        scratch_shapes=[dma((SLOTS, LAYERS))],
        compiler_params=pltpu.CompilerParams(vmem_limit_bytes=16 * MIB),
    )(owner_map, gathered, part)


def solution(mesh):
    in_specs = (
        P(None, "replica", None, "tensor"),
        P(None, "tensor", None),
        P(None, "tensor", "replica"),
        P(None, "tensor", "replica"),
        P(),
        P(),
        P(None, "replica", None, None, None),
        P(None, "replica", "tensor", None, None),
        P(None, "replica", "tensor", None, None),
        P("replica"),
    )
    out_specs = (P(None, "tensor", None), P(None, "replica", None, "tensor", None))
    return jax.shard_map(
        on_device, mesh=mesh, in_specs=in_specs, out_specs=out_specs, check_vma=False
    )
```

```python
import functools
import math

import jax
import jax.numpy as jnp
import numpy as np
from jax import lax
from jax.experimental import pallas as pl
from jax.experimental.pallas import tpu as pltpu
from jax.sharding import PartitionSpec as P

MESH = pl.DeviceIdType.MESH
ROPE_BASE = 1000000.0
MIB = 1 << 20
NEG = -1e30

LAYERS = 2
STEPS = 4
ROWS = 512
HD = 128
SLOTS = 16
PEERS = 16
HEADS = 64
KVH = 8
QROWS = STEPS * HEADS
OWN = QROWS // PEERS
SPOTS = 512
COLS = SPOTS * KVH
WIDE = 1024
CHIPS = 8
CHUNKS = 4
HALF = ROWS * LAYERS // CHUNKS
EXP_SCALE = HD**-0.5 * math.log2(math.e)


def place():
    replica = lax.axis_index("replica")
    return replica // 8, (replica // 2) % 4, replica % 2, lax.axis_index("tensor")


def slot_of(xh, y, c):
    return (xh * 4 + y) * 2 + c


def gather_kernel(
    map_hbm, len_ref, hid_hbm, res_hbm, code_hbm, scale_hbm, bias_hbm, inv_hbm, q_hbm, k_hbm, v_hbm,
    gat, out_ref, map_out,
    map_ref, hid_ref, res, code_ref, scale_ref, bias_ref, inv_ref, q_ref, kbuf, vbuf,
    hall, qp, sbuf, top, peak, total, acc, side, asend, arecv, part, proj, psend, precv,
    load_sem, r_sem, sib_r_sem, own_sem, y2_sem, cross_sem, far_sem, sib_sem,
    h_r_sem, h_sem, token_sem, as_sem, ar_sem, part_sem, part_r_sem, ps_sem, pr_sem,
):
    xh, y, c, t = place()
    me = slot_of(xh, y, c)

    pairs = [
        (map_hbm, map_ref), (scale_hbm, scale_ref), (code_hbm, code_ref), (res_hbm, res),
        (hid_hbm, hid_ref), (q_hbm, q_ref), (k_hbm, kbuf), (v_hbm, vbuf),
        (bias_hbm, bias_ref), (inv_hbm, inv_ref),
    ]
    loads = [pltpu.make_async_copy(a, b, load_sem.at[i]) for i, (a, b) in enumerate(pairs)]
    for load in loads:
        load.start()

    def loop(low, high, body):
        def step(j, carry):
            body(j)
            return carry

        lax.fori_loop(low, high, step, 0)

    def device(x2, y2, c2):
        return (slot_of(x2, y2, c2), t)

    y_up, y_down, y_far = (y + 1) % 4, (y + 3) % 4, (y + 2) % 4
    to_up, to_down = device(xh, y_up, c), device(xh, y_down, c)
    to_x, to_sib = device(1 - xh, y, c), device(xh, y, 1 - c)

    barrier = pltpu.get_barrier_semaphore()
    chip = xh * 4 + y
    pl.semaphore_signal(barrier, inc=1, device_id=to_sib, device_id_type=MESH)

    def chip_device(k):
        return (((chip + k) % CHIPS) * 2 + c, t)

    def greet_chip(k):
        pl.semaphore_signal(barrier, inc=1, device_id=chip_device(k), device_id_type=MESH)

    loop(1, CHIPS, greet_chip)

    def greet(k):
        pl.semaphore_signal(barrier, inc=1, device_id=(me, k), device_id_type=MESH)

    loop(t + 1, PEERS, greet)

    loads[0].wait()
    group = jnp.int32(0)
    for g in range(SLOTS):
        group = group + jnp.where(map_ref[g] == me, g, 0)
        map_out[g] = map_ref[g]
    for load in loads[1:5]:
        load.wait()
    group_all = jnp.broadcast_to(group.astype(jnp.float32), (HD, HD)).astype(jnp.bfloat16)
    for layer in range(LAYERS):
        for p in range(ROWS // HD):
            rows = pl.ds(p * HD, HD)
            line = scale_ref[pl.ds(layer, 1), rows].astype(jnp.float32)
            column = jnp.transpose(jnp.broadcast_to(line, (HD, HD)))
            code = code_ref[layer, rows, :].astype(jnp.float32)
            base = res[layer, rows, :HD]
            for g in range(1, SLOTS):
                base = jnp.where(group_all == g, res[layer, rows, g * HD : (g + 1) * HD], base)
            base = base.astype(jnp.float32)
            gat[me, layer, rows, :] = (base + code * column).astype(jnp.bfloat16)
    halves = [
        hid_ref[layer, 0, :, h * 256 : (h + 1) * 256].astype(jnp.float32)
        for h in range(2)
        for layer in range(LAYERS)
    ]
    hall[c, chip] = jnp.concatenate(halves, axis=0).astype(jnp.bfloat16)

    pl.semaphore_wait(barrier, CHIPS + t)

    def copy_of(src, dst, s_sem, rr_sem, target):
        return pltpu.make_async_remote_copy(
            src_ref=src, dst_ref=dst, send_sem=s_sem, recv_sem=rr_sem,
            device_id=target, device_id_type=MESH,
        )

    s_up, s_down = slot_of(xh, y_up, c), slot_of(xh, y_down, c)
    s_far, s_x = slot_of(xh, y_far, c), slot_of(1 - xh, y, c)
    x_up, x_down = slot_of(1 - xh, y_up, c), slot_of(1 - xh, y_down, c)
    x_far = slot_of(1 - xh, y_far, c)
    others = [s_up, s_down, s_x, s_far, x_up, x_down, x_far]

    def flip(slot):
        return slot + 1 - 2 * c

    def h_copy(k):
        return copy_of(
            hall.at[c, chip], hall.at[c, chip], h_sem.at[k], h_r_sem.at[chip], chip_device(k)
        )

    def h_arrived(k):
        other = (chip + k) % CHIPS
        copy_of(
            hall.at[c, other], hall.at[c, other], h_sem.at[k], h_r_sem.at[other], to_sib
        ).wait_recv()

    def h_sib(core):
        return copy_of(hall.at[core], hall.at[core], h_sem.at[0], h_r_sem.at[CHIPS], to_sib)

    def rows_of(slot, j, count):
        return gat.at[slot, j // 2, pl.ds(pl.multiple_of((j % 2) * HALF, HALF), HALF * count), :]

    def send(slot, j, sem, target):
        ref = rows_of(slot, j, 1)
        return copy_of(ref, ref, sem, r_sem.at[slot, j], target)

    def arrived(slot, j):
        send(slot, j, r_sem.at[slot, j], to_sib).wait_recv()

    def sib_copy(i, slot, layer):
        ref = gat.at[slot, layer]
        return copy_of(ref, ref, sib_sem.at[i, layer], sib_r_sem.at[slot, layer], to_sib)

    def sib_send(i, layer):
        sib_copy(i, others[i - 1] if i else me, layer).start()

    def own_copies(j):
        return [
            send(me, j, own_sem.at[0, j], to_up),
            send(me, j, own_sem.at[1, j], to_down),
            send(me, j, own_sem.at[2, j], to_x),
        ]

    def onward(j):
        up = 1 - 2 * (j % 2)
        return slot_of(xh, (y + 4 - up) % 4, c), device(xh, (y + 4 + up) % 4, c)

    def y2_copy(j):
        slot, target = onward(j)
        return send(slot, j, y2_sem.at[j], target)

    def cross_copies(j):
        return [send(s_x, j, cross_sem.at[0, j], to_up), send(s_x, j, cross_sem.at[1, j], to_down)]

    def far_copy(j):
        return send(s_far, j, far_sem.at[j], to_x)

    def y2_step(j):
        slot, _ = onward(j)
        arrived(slot, j)
        y2_copy(j).start()

    def cross_step(j):
        arrived(s_x, j)
        for copy in cross_copies(j):
            copy.start()

    loop(1, CHIPS, lambda k: h_copy(k).start())

    def own_step(j):
        for copy in own_copies(j):
            copy.start()

    loop(0, CHUNKS - 1, own_step)

    def answer(k):
        pl.semaphore_signal(token_sem, inc=1, device_id=(me, k), device_id_type=MESH)

    loop(0, t, answer)

    loads[5].wait()
    row = lax.broadcasted_iota(jnp.int32, (QROWS, QROWS), 0)
    col = lax.broadcasted_iota(jnp.int32, (QROWS, QROWS), 1)
    source = ((row // STEPS) % STEPS) * HEADS + (row // OWN) * STEPS + row % STEPS
    pick = jnp.where(col == source, 1.0, 0.0).astype(jnp.bfloat16)
    for layer in range(LAYERS):
        qp[layer] = jnp.dot(pick, q_ref[layer], preferred_element_type=jnp.float32).astype(
            jnp.bfloat16
        )
    length = len_ref[0]
    limit = (length - t * SPOTS) * KVH
    lanes = lax.broadcasted_iota(jnp.int32, (1, WIDE), 1)
    lane = lax.broadcasted_iota(jnp.int32, (QROWS, HD), 1)
    valid = lane % KVH == lax.broadcasted_iota(jnp.int32, (QROWS, HD), 0) // (QROWS // KVH)

    def scores(layer):
        top[...] = jnp.full((QROWS, HD), NEG, jnp.float32)
        for n in range(COLS // WIDE):
            first = n * WIDE
            s = lax.dot_general(
                qp[layer], kbuf[layer, first : first + WIDE, :], (((1,), (1,)), ((), ())),
                preferred_element_type=jnp.float32,
            )
            s = s + jnp.where(lanes + first < limit, 0.0, NEG)
            sbuf[:, first : first + WIDE] = s
            high = top[...]
            for i in range(WIDE // HD):
                high = jnp.maximum(high, s[:, i * HD : (i + 1) * HD])
            top[...] = high
        high = jnp.max(jnp.where(valid, top[...], NEG), axis=1, keepdims=True)
        peak[...] = jnp.broadcast_to(high, (QROWS, HD))
        top[...] = jnp.where(valid, high, -NEG)

    def values(layer):
        total[...] = jnp.zeros((QROWS, HD), jnp.float32)
        acc[...] = jnp.zeros((QROWS, HD), jnp.float32)
        for n in range(COLS // WIDE):
            first = n * WIDE
            high = top[...]
            added = total[...]
            pieces = []
            for i in range(WIDE // HD):
                e = jnp.exp2((sbuf[:, first + i * HD : first + (i + 1) * HD] - high) * EXP_SCALE)
                added = added + e
                pieces.append(e.astype(jnp.bfloat16))
            total[...] = added
            acc[...] += jnp.dot(
                jnp.concatenate(pieces, axis=1), vbuf[layer, first : first + WIDE, :],
                preferred_element_type=jnp.float32,
            )
        whole = jnp.broadcast_to(jnp.sum(total[...], axis=1, keepdims=True), (QROWS, HD))
        asend[:, layer * OWN : (layer + 1) * OWN, :] = (
            (acc[...] / whole).astype(jnp.bfloat16).reshape(PEERS, OWN, HD)
        )
        rest = peak[...] * EXP_SCALE + jnp.log(whole) * math.log2(math.e)
        kept = side[...] if layer else jnp.zeros((QROWS, HD), jnp.float32)
        for i in range(3):
            term = rest.astype(jnp.bfloat16).astype(jnp.float32)
            rest = rest - term
            kept = jnp.where(lane == 3 * layer + i, term, kept)
        side[...] = kept

    loads[6].wait()
    scores(0)
    loads[7].wait()
    values(0)
    own_step(CHUNKS - 1)
    for layer in range(LAYERS):
        sib_send(0, layer)
    loop(1, CHIPS, h_arrived)
    h_sib(c).start()
    scores(1)
    loop(0, 2, y2_step)
    h_sib(1 - c).wait_recv()

    rows8 = lax.broadcasted_iota(jnp.int32, (SLOTS, LAYERS * STEPS, HD), 1)
    product = []
    for layer in range(LAYERS):
        halves = [
            jnp.dot(
                hall[...].reshape(SLOTS * 16, 256), gat[me, layer, h * 256 : (h + 1) * 256, :],
                preferred_element_type=jnp.float32,
            ).reshape(SLOTS, 16, HD)
            for h in range(2)
        ]
        product.append(halves[0][:, :8] + halves[1][:, 8:])
    part[...] = jnp.where(rows8 < STEPS, product[0], product[1])

    def part_copy(k):
        target = (me + k) % SLOTS
        return copy_of(
            part.at[(target % 2) * CHIPS + target // 2], proj.at[me],
            part_sem.at[target], part_r_sem.at[me], (target, t),
        )

    def part_arrived(k):
        other = (me + k) % SLOTS
        copy_of(
            part.at[other], proj.at[other], part_sem.at[other], part_r_sem.at[other], to_sib
        ).wait_recv()

    loop(1, SLOTS, lambda k: part_copy(k).start())
    proj[me] = part[c * CHIPS + chip]

    values(1)
    asend[:, 2 * OWN :, :] = side[...].astype(jnp.bfloat16).reshape(PEERS, OWN, HD)
    loop(2, CHUNKS, y2_step)
    loop(0, 2, cross_step)

    def peer_copy(src, dst, s_sem, rr_sem, k):
        target = (t + k) % PEERS
        return copy_of(src(target), dst.at[t], s_sem.at[target], rr_sem.at[t], (me, target))

    def peer_arrived(src, dst, s_sem, rr_sem, k):
        other = (t + k) % PEERS
        copy_of(
            src(other), dst.at[other], s_sem.at[other], rr_sem.at[other], (me, other)
        ).wait_recv()

    attention = (lambda target: asend.at[target], arecv, as_sem, ar_sem)
    project = (lambda target: psend.at[target // 2], precv, ps_sem, pr_sem)
    loop(1, SLOTS, part_arrived)
    for g in range(SLOTS):
        slot_all = jnp.broadcast_to(map_ref[g], (LAYERS * STEPS, HD))
        line = proj[0]
        for slot in range(1, SLOTS):
            line = jnp.where(slot_all == slot, proj[slot], line)
        psend[g // 2, (g % 2) * 8 : (g % 2) * 8 + 8, :] = line
    precv[t] = psend[t // 2]
    arecv[t] = asend[t]

    def send_peers():
        pl.when(t < PEERS - 1)(lambda: pl.semaphore_wait(token_sem, PEERS - 1 - t))
        loop(1, PEERS, lambda k: peer_copy(*project, k).start())
        loop(1, PEERS, lambda k: peer_copy(*attention, k).start())

    pl.when(t >= PEERS // 2)(send_peers)
    loop(2, CHUNKS, cross_step)

    def opposite_step(j):
        arrived(slot_of(xh, (y + 4 + 1 - 2 * (j % 2)) % 4, c), j)

    def far_step(j):
        arrived(s_far, j)
        far_copy(j).start()

    loop(0, CHUNKS, far_step)
    pl.when(t < PEERS // 2)(send_peers)
    loop(0, CHUNKS, opposite_step)
    for layer in range(LAYERS):
        for i in range(4):
            sib_send(i + 1, layer)

    for load in loads[8:]:
        load.wait()
    turn_row = lax.broadcasted_iota(jnp.int32, (LAYERS * STEPS, HD), 0)
    turn_lane = lax.broadcasted_iota(jnp.int32, (LAYERS * STEPS, HD), 1)
    angle = (length + turn_row % STEPS).astype(jnp.float32) * inv_ref[...]
    cosine = jnp.cos(angle)
    sine = jnp.where(turn_lane < HD // 2, -1.0, 1.0) * jnp.sin(angle)
    head = t // 2
    bias = bias_ref[:, pl.ds(pl.multiple_of(head * 2 * HD, 2 * HD), 2 * HD)].astype(jnp.float32)

    for layer in range(LAYERS):
        for i, slot in ((5, x_up), (6, x_down), (7, x_far)):
            loop(2 * layer, 2 * layer + 2, lambda j, slot=slot: arrived(slot, j))
            sib_send(i, layer)

    loop(1, PEERS, lambda k: peer_arrived(*attention, k))
    joined = []
    sides = [arecv[p, 2 * OWN :, :].astype(jnp.float32) for p in range(PEERS)]
    for layer in range(LAYERS):
        logs = [sum(x[:, 3 * layer + i : 3 * layer + i + 1] for i in range(3)) for x in sides]
        high = functools.reduce(jnp.maximum, logs)
        whole = jnp.zeros((OWN, 1), jnp.float32)
        summed = jnp.zeros((OWN, HD), jnp.float32)
        for p in range(PEERS):
            factor = jnp.exp2(logs[p] - high)
            whole = whole + factor
            summed = summed + factor * arecv[p, layer * OWN : (layer + 1) * OWN, :].astype(jnp.float32)
        joined.append((high, whole, summed))

    loop(1, PEERS, lambda k: peer_arrived(*project, k))
    projected = precv[0]
    for p in range(1, PEERS):
        projected = projected + precv[p]
    projected = projected * (ROWS * PEERS) ** -0.5

    def biased(kind):
        lines = [
            jnp.broadcast_to(bias[layer : layer + 1, kind * HD : (kind + 1) * HD], (8, HD))
            for layer in range(LAYERS)
        ]
        return projected[kind * 8 : kind * 8 + 8] + jnp.where(turn_row < STEPS, lines[0], lines[1])

    key = biased(0)
    key = (key * cosine + pltpu.roll(key, HD // 2, 1) * sine).astype(jnp.bfloat16)
    value = biased(1).astype(jnp.bfloat16)
    row = lax.broadcasted_iota(jnp.int32, (OWN, LAYERS * STEPS), 0)
    col = lax.broadcasted_iota(jnp.int32, (OWN, LAYERS * STEPS), 1)
    for layer in range(LAYERS):
        query = qp[layer, pl.ds(pl.multiple_of(t * OWN, OWN), OWN), :]
        s = lax.dot_general(
            query, key, (((1,), (1,)), ((), ())), preferred_element_type=jnp.float32
        )
        allowed = (col // STEPS == layer) & (col % STEPS <= row // STEPS)
        s = jnp.where(allowed, s * EXP_SCALE, NEG)
        high, whole, summed = joined[layer]
        top_all = jnp.maximum(high, jnp.max(s, axis=1, keepdims=True))
        e = jnp.exp2(s - top_all)
        factor = jnp.exp2(high - top_all)
        whole = whole * factor + jnp.sum(e, axis=1, keepdims=True)
        summed = summed * factor + jnp.dot(
            e.astype(jnp.bfloat16), value, preferred_element_type=jnp.float32
        )
        result = (summed / whole).astype(jnp.bfloat16)
        for step in range(STEPS):
            out_ref[layer, 0, step] = result[step * 4 : step * 4 + 4]

    for i, slot in enumerate([me] + others):
        for layer in range(LAYERS):
            sib_copy(i, flip(slot), layer).wait_recv()
            sib_copy(i, slot, layer).wait_send()

    def sent(j):
        for copy in own_copies(j) + cross_copies(j) + [y2_copy(j), far_copy(j)]:
            copy.wait_send()

    loop(0, CHUNKS, sent)
    loop(1, CHIPS, lambda k: h_copy(k).wait_send())
    h_sib(c).wait_send()
    loop(1, SLOTS, lambda k: part_copy(k).wait_send())
    loop(1, PEERS, lambda k: peer_copy(*attention, k).wait_send())
    loop(1, PEERS, lambda k: peer_copy(*project, k).wait_send())


def place_kernel(map_ref, gat, part, out_hbm, part_out, sem, part_sem):
    last = pltpu.make_async_copy(part, part_out, part_sem)
    last.start()
    copies = []
    for group in range(SLOTS):
        for layer in range(LAYERS):
            copy = pltpu.make_async_copy(
                gat.at[map_ref[group], layer],
                out_hbm.at[layer, :, pl.ds(group * HD, HD)],
                sem.at[group, layer],
            )
            copy.start()
            copies.append(copy)
    for copy in copies:
        copy.wait()
    last.wait()


def on_device(
    hidden, resident, delta_codes, scales, owner_map, key_value_bias, queries, key_cache,
    value_cache, lengths,
):
    inverse = (ROPE_BASE ** (-2.0 * np.arange(HD // 2) / HD)).astype(np.float32)
    inverse = jnp.asarray(np.concatenate([inverse, inverse])[None, :])
    smem = pl.BlockSpec(memory_space=pltpu.SMEM)
    vmem = pl.BlockSpec(memory_space=pltpu.VMEM)
    hbm = pl.BlockSpec(memory_space=pltpu.HBM)
    anywhere = pl.BlockSpec(memory_space=pl.ANY)
    dma = pltpu.SemaphoreType.DMA
    f32, bf16 = jnp.float32, jnp.bfloat16
    part_shape = (LAYERS, 1, STEPS, HEADS // PEERS, HD)
    arrays = (
        owner_map, lengths, hidden, resident, delta_codes,
        scales.reshape(LAYERS, ROWS), key_value_bias, inverse,
        queries.reshape(LAYERS, QROWS, HD),
        key_cache.reshape(LAYERS, COLS, HD), value_cache.reshape(LAYERS, COLS, HD),
    )
    gathered, part, chosen = pl.pallas_call(
        gather_kernel,
        out_shape=(
            pltpu.VMEM((SLOTS, LAYERS, ROWS, HD), bf16),
            jax.ShapeDtypeStruct(part_shape, bf16),
            pltpu.SMEM((SLOTS,), jnp.int32),
        ),
        in_specs=[hbm, smem] + [hbm] * 9,
        out_specs=(vmem, vmem, smem),
        scratch_shapes=[
            pltpu.SMEM((SLOTS,), jnp.int32),
            pltpu.VMEM((LAYERS, 1, STEPS, ROWS), bf16),
            pltpu.VMEM((LAYERS, ROWS, SLOTS * HD), bf16),
            pltpu.VMEM((LAYERS, ROWS, HD), bf16),
            pltpu.VMEM((LAYERS, ROWS), bf16),
            pltpu.VMEM((LAYERS, SLOTS * HD), bf16),
            pltpu.VMEM((1, HD), f32),
            pltpu.VMEM((LAYERS, QROWS, HD), bf16),
            pltpu.VMEM((LAYERS, COLS, HD), bf16),
            pltpu.VMEM((LAYERS, COLS, HD), bf16),
            pltpu.VMEM((2, CHIPS, 16, 256), bf16),
            pltpu.VMEM((LAYERS, QROWS, HD), bf16),
            pltpu.VMEM((QROWS, COLS), f32),
            pltpu.VMEM((QROWS, HD), f32),
            pltpu.VMEM((QROWS, HD), f32),
            pltpu.VMEM((QROWS, HD), f32),
            pltpu.VMEM((QROWS, HD), f32),
            pltpu.VMEM((QROWS, HD), f32),
            pltpu.VMEM((PEERS, 3 * OWN, HD), bf16),
            pltpu.VMEM((PEERS, 3 * OWN, HD), bf16),
            pltpu.VMEM((SLOTS, LAYERS * STEPS, HD), f32),
            pltpu.VMEM((SLOTS, LAYERS * STEPS, HD), f32),
            pltpu.VMEM((PEERS // 2, 16, HD), f32),
            pltpu.VMEM((PEERS, 16, HD), f32),
            dma((10,)),
            dma((SLOTS, CHUNKS)),
            dma((SLOTS, LAYERS)),
            dma((3, CHUNKS)),
            dma((CHUNKS,)),
            dma((2, CHUNKS)),
            dma((CHUNKS,)),
            dma((8, LAYERS)),
            dma((CHIPS + 1,)),
            dma((CHIPS,)),
            pltpu.SemaphoreType.REGULAR,
            dma((PEERS,)),
            dma((PEERS,)),
            dma((SLOTS,)),
            dma((SLOTS,)),
            dma((PEERS,)),
            dma((PEERS,)),
        ],
        compiler_params=pltpu.CompilerParams(
            collective_id=0, has_side_effects=True, vmem_limit_bytes=40 * MIB
        ),
    )(*(a if a.size == 1 else pltpu.with_memory_space_constraint(a, pltpu.HBM) for a in arrays))
    return pl.pallas_call(
        place_kernel,
        out_shape=(
            jax.ShapeDtypeStruct((LAYERS, ROWS, SLOTS * HD), bf16),
            jax.ShapeDtypeStruct(part_shape, bf16),
        ),
        in_specs=[smem, vmem, vmem],
        out_specs=(anywhere, anywhere),
        scratch_shapes=[dma((SLOTS, LAYERS)), dma(())],
        compiler_params=pltpu.CompilerParams(vmem_limit_bytes=16 * MIB),
    )(chosen, gathered, part)


def solution(mesh):
    in_specs = (
        P(None, "replica", None, "tensor"),
        P(None, "tensor", None),
        P(None, "tensor", "replica"),
        P(None, "tensor", "replica"),
        P(),
        P(),
        P(None, "replica", None, None, None),
        P(None, "replica", "tensor", None, None),
        P(None, "replica", "tensor", None, None),
        P("replica"),
    )
    out_specs = (P(None, "tensor", None), P(None, "replica", None, "tensor", None))
    return jax.shard_map(
        on_device, mesh=mesh, in_specs=in_specs, out_specs=out_specs, check_vma=False
    )
```

```python
import functools
import math

import jax
import jax.numpy as jnp
import numpy as np
from jax import lax
from jax.experimental import pallas as pl
from jax.experimental.pallas import tpu as pltpu
from jax.sharding import PartitionSpec as P

MESH = pl.DeviceIdType.MESH
ROPE_BASE = 1000000.0
MIB = 1 << 20
NEG = -1e30

LAYERS = 2
STEPS = 4
ROWS = 512
HD = 128
SLOTS = 16
PEERS = 16
RANKS = 8
HEADS = 64
KVH = 8
QROWS = STEPS * HEADS
OWN = QROWS // PEERS
SPOTS = 512
COLS = SPOTS * KVH
WIDE = 1024
CHIPS = 8
CHUNKS = 4
HALF = ROWS * LAYERS // CHUNKS
EXP_SCALE = HD**-0.5 * math.log2(math.e)


def place():
    replica = lax.axis_index("replica")
    return replica // 8, (replica // 2) % 4, replica % 2, lax.axis_index("tensor")


def slot_of(xh, y, c):
    return (xh * 4 + y) * 2 + c


def gather_kernel(
    map_hbm, len_ref, hid_hbm, res_hbm, code_hbm, scale_hbm, bias_hbm, inv_hbm, q_hbm, k_hbm, v_hbm,
    gat, out_ref, map_out,
    map_ref, hid_ref, res, code_ref, scale_ref, bias_ref, inv_ref, q_ref, kbuf, vbuf,
    hall, qp, sbuf, top, peak, total, acc, side, asend, arecv, part, proj, psend, precv, pair_own, pair_in,
    load_sem, r_sem, sib_r_sem, own_sem, y2_sem, cross_sem, far_sem, sib_sem,
    h_r_sem, h_sem, token_sem, as_sem, ar_sem, part_sem, part_r_sem, ps_sem, pr_sem, pair_sem,
):
    xh, y, c, t = place()
    me = slot_of(xh, y, c)

    pairs = [
        (map_hbm, map_ref), (hid_hbm, hid_ref), (scale_hbm, scale_ref), (code_hbm, code_ref),
    ]
    for j in range(CHUNKS):
        rows = pl.ds((j % 2) * HALF, HALF)
        pairs.append((res_hbm.at[j // 2, rows, :], res.at[j // 2, rows, :]))
    pairs += [
        (q_hbm, q_ref), (k_hbm, kbuf), (v_hbm, vbuf), (bias_hbm, bias_ref), (inv_hbm, inv_ref),
    ]
    loads = [pltpu.make_async_copy(a, b, load_sem.at[i]) for i, (a, b) in enumerate(pairs)]
    load_map, load_hid, load_scale, load_code = loads[:4]
    load_res, (load_q, load_k, load_v, load_bias, load_inv) = loads[4:8], loads[8:]
    for load in loads[:8]:
        load.start()

    def loop(low, high, body):
        def step(j, carry):
            body(j)
            return carry

        lax.fori_loop(low, high, step, 0)

    def device(x2, y2, c2):
        return (slot_of(x2, y2, c2), t)

    y_up, y_down, y_far = (y + 1) % 4, (y + 3) % 4, (y + 2) % 4
    to_up, to_down = device(xh, y_up, c), device(xh, y_down, c)
    to_x, to_sib = device(1 - xh, y, c), device(xh, y, 1 - c)

    barrier = pltpu.get_barrier_semaphore()
    chip = xh * 4 + y
    pl.semaphore_signal(barrier, inc=1, device_id=to_sib, device_id_type=MESH)

    def chip_device(k):
        return (((chip + k) % CHIPS) * 2 + c, t)

    def greet_chip(k):
        pl.semaphore_signal(barrier, inc=1, device_id=chip_device(k), device_id_type=MESH)

    loop(1, CHIPS, greet_chip)

    z, xl = t // 2, t % 2
    low, high_rank = z < RANKS // 2, z >= RANKS // 2

    def rank_device(k):
        return (me, k * 2 + xl)

    to_pair = (me, z * 2 + 1 - xl)

    def greet(k):
        pl.semaphore_signal(barrier, inc=1, device_id=rank_device(k), device_id_type=MESH)

    loop(z + 1, RANKS, greet)

    @pl.when(xl == 0)
    def _():
        pl.semaphore_signal(barrier, inc=1, device_id=to_pair, device_id_type=MESH)

    load_map.wait()
    group = jnp.int32(0)
    for g in range(SLOTS):
        group = group + jnp.where(map_ref[g] == me, g, 0)
        map_out[g] = map_ref[g]
    group_all = jnp.broadcast_to(group.astype(jnp.float32), (HD, HD)).astype(jnp.bfloat16)

    def own_block(j):
        load_res[j].wait()
        layer = j // 2
        for p in range(HALF // HD):
            rows = pl.ds((j % 2) * HALF + p * HD, HD)
            line = scale_ref[pl.ds(layer, 1), rows].astype(jnp.float32)
            column = jnp.transpose(jnp.broadcast_to(line, (HD, HD)))
            code = code_ref[layer, rows, :].astype(jnp.float32)
            base = res[layer, rows, :HD]
            for g in range(1, SLOTS):
                base = jnp.where(group_all == g, res[layer, rows, g * HD : (g + 1) * HD], base)
            base = base.astype(jnp.float32)
            gat[me, layer, rows, :] = (base + code * column).astype(jnp.bfloat16)

    load_hid.wait()
    halves = [
        hid_ref[layer, 0, :, h * 256 : (h + 1) * 256].astype(jnp.float32)
        for h in range(2)
        for layer in range(LAYERS)
    ]
    hall[c, chip] = jnp.concatenate(halves, axis=0).astype(jnp.bfloat16)

    load_scale.wait()
    load_code.wait()
    own_block(0)
    own_block(1)
    for load in loads[8:]:
        load.start()

    pl.semaphore_wait(barrier, CHIPS + z + xl)

    def copy_of(src, dst, s_sem, rr_sem, target):
        return pltpu.make_async_remote_copy(
            src_ref=src, dst_ref=dst, send_sem=s_sem, recv_sem=rr_sem,
            device_id=target, device_id_type=MESH,
        )

    s_up, s_down = slot_of(xh, y_up, c), slot_of(xh, y_down, c)
    s_far, s_x = slot_of(xh, y_far, c), slot_of(1 - xh, y, c)
    x_up, x_down = slot_of(1 - xh, y_up, c), slot_of(1 - xh, y_down, c)
    x_far = slot_of(1 - xh, y_far, c)
    others = [s_up, s_down, s_x, s_far, x_up, x_down, x_far]

    def flip(slot):
        return slot + 1 - 2 * c

    def h_copy(k):
        return copy_of(
            hall.at[c, chip], hall.at[c, chip], h_sem.at[k], h_r_sem.at[chip], chip_device(k)
        )

    def h_arrived(k):
        other = (chip + k) % CHIPS
        copy_of(
            hall.at[c, other], hall.at[c, other], h_sem.at[k], h_r_sem.at[other], to_sib
        ).wait_recv()

    def h_sib(core):
        return copy_of(hall.at[core], hall.at[core], h_sem.at[0], h_r_sem.at[CHIPS], to_sib)

    def rows_of(slot, j, count):
        return gat.at[slot, j // 2, pl.ds(pl.multiple_of((j % 2) * HALF, HALF), HALF * count), :]

    def send(slot, j, sem, target):
        ref = rows_of(slot, j, 1)
        return copy_of(ref, ref, sem, r_sem.at[slot, j], target)

    def arrived(slot, j):
        send(slot, j, r_sem.at[slot, j], to_sib).wait_recv()

    def sib_copy(i, slot, layer):
        ref = gat.at[slot, layer]
        return copy_of(ref, ref, sib_sem.at[i, layer], sib_r_sem.at[slot, layer], to_sib)

    def sib_send(i, layer):
        sib_copy(i, others[i - 1] if i else me, layer).start()

    def own_copies(j):
        return [
            send(me, j, own_sem.at[0, j], to_up),
            send(me, j, own_sem.at[1, j], to_down),
            send(me, j, own_sem.at[2, j], to_x),
        ]

    def onward(j):
        up = 1 - 2 * (j % 2)
        return slot_of(xh, (y + 4 - up) % 4, c), device(xh, (y + 4 + up) % 4, c)

    def y2_copy(j):
        slot, target = onward(j)
        return send(slot, j, y2_sem.at[j], target)

    def cross_copies(j):
        return [send(s_x, j, cross_sem.at[0, j], to_up), send(s_x, j, cross_sem.at[1, j], to_down)]

    def far_copy(j):
        return send(s_far, j, far_sem.at[j], to_x)

    def y2_step(j):
        slot, _ = onward(j)
        arrived(slot, j)
        y2_copy(j).start()

    def cross_step(j):
        arrived(s_x, j)
        for copy in cross_copies(j):
            copy.start()

    loop(1, CHIPS, lambda k: h_copy(k).start())

    def own_step(j):
        for copy in own_copies(j):
            copy.start()

    loop(0, 2, own_step)
    own_block(2)
    own_step(2)
    own_block(3)
    pl.when(low)(functools.partial(own_step, 3))

    def answer(k):
        pl.semaphore_signal(token_sem, inc=1, device_id=rank_device(k), device_id_type=MESH)

    loop(0, z, answer)

    @pl.when(xl == 1)
    def _():
        pl.semaphore_signal(token_sem, inc=1, device_id=to_pair, device_id_type=MESH)

    load_q.wait()
    row = lax.broadcasted_iota(jnp.int32, (QROWS, QROWS), 0)
    col = lax.broadcasted_iota(jnp.int32, (QROWS, QROWS), 1)
    source = ((row // STEPS) % STEPS) * HEADS + (row // OWN) * STEPS + row % STEPS
    pick = jnp.where(col == source, 1.0, 0.0).astype(jnp.bfloat16)
    for layer in range(LAYERS):
        qp[layer] = jnp.dot(pick, q_ref[layer], preferred_element_type=jnp.float32).astype(
            jnp.bfloat16
        )
    length = len_ref[0]
    limit = (length - t * SPOTS) * KVH
    lanes = lax.broadcasted_iota(jnp.int32, (1, WIDE), 1)
    lane = lax.broadcasted_iota(jnp.int32, (QROWS, HD), 1)
    valid = lane % KVH == lax.broadcasted_iota(jnp.int32, (QROWS, HD), 0) // (QROWS // KVH)

    def scores(layer):
        top[...] = jnp.full((QROWS, HD), NEG, jnp.float32)
        for n in range(COLS // WIDE):
            first = n * WIDE
            s = lax.dot_general(
                qp[layer], kbuf[layer, first : first + WIDE, :], (((1,), (1,)), ((), ())),
                preferred_element_type=jnp.float32,
            )
            s = s + jnp.where(lanes + first < limit, 0.0, NEG)
            sbuf[:, first : first + WIDE] = s
            high = top[...]
            for i in range(WIDE // HD):
                high = jnp.maximum(high, s[:, i * HD : (i + 1) * HD])
            top[...] = high
        high = jnp.max(jnp.where(valid, top[...], NEG), axis=1, keepdims=True)
        peak[...] = jnp.broadcast_to(high, (QROWS, HD))
        top[...] = jnp.where(valid, high, -NEG)

    def values(layer):
        total[...] = jnp.zeros((QROWS, HD), jnp.float32)
        acc[...] = jnp.zeros((QROWS, HD), jnp.float32)
        for n in range(COLS // WIDE):
            first = n * WIDE
            high = top[...]
            added = total[...]
            pieces = []
            for i in range(WIDE // HD):
                e = jnp.exp2((sbuf[:, first + i * HD : first + (i + 1) * HD] - high) * EXP_SCALE)
                added = added + e
                pieces.append(e.astype(jnp.bfloat16))
            total[...] = added
            acc[...] += jnp.dot(
                jnp.concatenate(pieces, axis=1), vbuf[layer, first : first + WIDE, :],
                preferred_element_type=jnp.float32,
            )
        whole = jnp.broadcast_to(jnp.sum(total[...], axis=1, keepdims=True), (QROWS, HD))
        asend[:, layer * 2 * OWN : (layer + 1) * 2 * OWN, :] = (
            (acc[...] / whole).astype(jnp.bfloat16).reshape(RANKS, 2 * OWN, HD)
        )
        rest = peak[...] * EXP_SCALE + jnp.log(whole) * math.log2(math.e)
        kept = side[...] if layer else jnp.zeros((QROWS, HD), jnp.float32)
        for i in range(3):
            term = rest.astype(jnp.bfloat16).astype(jnp.float32)
            rest = rest - term
            kept = jnp.where(lane == 3 * layer + i, term, kept)
        side[...] = kept

    def rank_copy(src, dst, s_sem, rr_sem, k):
        target = (z + k) % RANKS
        return copy_of(
            src(target), dst(z), s_sem.at[target], rr_sem.at[z], rank_device(target)
        )

    def rank_arrived(src, dst, s_sem, rr_sem, k):
        other = (z + k) % RANKS
        copy_of(
            src(other), dst(other), s_sem.at[other], rr_sem.at[other], rank_device(other)
        ).wait_recv()

    def run_of(ref, layer):
        return lambda rank: ref.at[rank, 0:32] if layer == 0 else ref.at[rank, 32:80]

    attention = [
        (run_of(asend, layer), run_of(arecv, layer), as_sem.at[layer], ar_sem.at[layer])
        for layer in range(LAYERS)
    ]
    project = (lambda rank: psend.at[rank], lambda rank: precv.at[rank], ps_sem, pr_sem)

    def answered():
        answers = (RANKS - 1 - z) + (1 - xl)
        pl.when(answers > 0)(lambda: pl.semaphore_wait(token_sem, answers))

    def send_attention(layer):
        loop(1, RANKS, lambda k: rank_copy(*attention[layer], k).start())

    def send_project():
        loop(1, RANKS, lambda k: rank_copy(*project, k).start())

    load_k.wait()
    scores(0)
    loop(1, CHIPS, h_arrived)
    h_sib(c).start()
    load_v.wait()
    values(0)

    @pl.when(high_rank)
    def _():
        answered()
        send_attention(0)

    for layer in range(LAYERS):
        sib_send(0, layer)
    pl.when(low)(lambda: loop(0, 2, y2_step))
    h_sib(1 - c).wait_recv()

    rows8 = lax.broadcasted_iota(jnp.int32, (SLOTS, LAYERS * STEPS, HD), 1)
    product = []
    for layer in range(LAYERS):
        halves = [
            jnp.dot(
                hall[...].reshape(SLOTS * 16, 256), gat[me, layer, h * 256 : (h + 1) * 256, :],
                preferred_element_type=jnp.float32,
            ).reshape(SLOTS, 16, HD)
            for h in range(2)
        ]
        product.append(halves[0][:, :8] + halves[1][:, 8:])
    part[...] = jnp.where(rows8 < STEPS, product[0], product[1])

    def part_copy(k):
        target = (me + k) % SLOTS
        return copy_of(
            part.at[(target % 2) * CHIPS + target // 2], proj.at[me],
            part_sem.at[target], part_r_sem.at[me], (target, t),
        )

    def part_arrived(k):
        other = (me + k) % SLOTS
        copy_of(
            part.at[other], proj.at[other], part_sem.at[other], part_r_sem.at[other], to_sib
        ).wait_recv()

    loop(1, SLOTS, lambda k: part_copy(k).start())
    proj[me] = part[c * CHIPS + chip]

    @pl.when(high_rank)
    def _():
        own_step(3)
        loop(0, 2, y2_step)

    scores(1)
    values(1)
    notes = side[...].reshape(RANKS, 2 * OWN, HD)
    second = pltpu.roll(notes[:, OWN:].reshape(RANKS * OWN, HD), HD // 2, 1)
    lane3 = lax.broadcasted_iota(jnp.int32, (RANKS, OWN, HD), 2)
    notes = jnp.where(lane3 < HD // 2, notes[:, :OWN], second.reshape(RANKS, OWN, HD))
    asend[:, 4 * OWN :, :] = notes.astype(jnp.bfloat16)
    pl.when(high_rank)(lambda: send_attention(1))
    loop(2, CHUNKS, y2_step)
    loop(0, CHUNKS, cross_step)

    loop(1, SLOTS, part_arrived)
    for g in range(SLOTS):
        slot_all = jnp.broadcast_to(map_ref[g], (LAYERS * STEPS, HD))
        line = proj[0]
        for slot in range(1, SLOTS):
            line = jnp.where(slot_all == slot, proj[slot], line)
        psend[g // 2, (g % 2) * 8 : (g % 2) * 8 + 8, :] = line
    precv[z] = psend[z]
    arecv[z] = asend[z]

    pl.when(high_rank)(send_project)

    def opposite_step(j):
        arrived(slot_of(xh, (y + 4 + 1 - 2 * (j % 2)) % 4, c), j)

    def far_step(j):
        arrived(s_far, j)
        far_copy(j).start()

    loop(0, CHUNKS, far_step)

    @pl.when(low)
    def _():
        answered()
        send_project()
        send_attention(0)
        send_attention(1)

    loop(0, CHUNKS, opposite_step)
    for layer in range(LAYERS):
        for i in range(4):
            sib_send(i + 1, layer)

    load_bias.wait()
    load_inv.wait()
    turn_row = lax.broadcasted_iota(jnp.int32, (LAYERS * STEPS, HD), 0)
    turn_lane = lax.broadcasted_iota(jnp.int32, (LAYERS * STEPS, HD), 1)
    angle = (length + turn_row % STEPS).astype(jnp.float32) * inv_ref[...]
    cosine = jnp.cos(angle)
    sine = jnp.where(turn_lane < HD // 2, -1.0, 1.0) * jnp.sin(angle)
    head = t // 2
    bias = bias_ref[:, pl.ds(pl.multiple_of(head * 2 * HD, 2 * HD), 2 * HD)].astype(jnp.float32)

    def last_pieces():
        for layer in range(LAYERS):
            for i, slot in ((5, x_up), (6, x_down), (7, x_far)):
                loop(2 * layer, 2 * layer + 2, lambda j, slot=slot: arrived(slot, j))
                sib_send(i, layer)

    pl.when(low)(last_pieces)

    for layer in range(LAYERS):
        loop(1, RANKS, lambda k, layer=layer: rank_arrived(*attention[layer], k))
    lane32 = lax.broadcasted_iota(jnp.int32, (2 * OWN, HD), 1)
    sides = [arecv[p, 4 * OWN :, :].astype(jnp.float32) for p in range(RANKS)]
    notes = jnp.zeros((2 * OWN, HD), jnp.float32)
    for layer in range(LAYERS):
        logs = []
        for x in sides:
            firsts = (3 * layer, 3 * layer + HD // 2)
            columns = [sum(x[:, n + i : n + i + 1] for i in range(3)) for n in firsts]
            logs.append(jnp.concatenate(columns, axis=0))
        high = functools.reduce(jnp.maximum, logs)
        whole = jnp.zeros((2 * OWN, 1), jnp.float32)
        summed = jnp.zeros((2 * OWN, HD), jnp.float32)
        rows = slice(layer * 2 * OWN, (layer + 1) * 2 * OWN)
        for p in range(RANKS):
            factor = jnp.exp2(logs[p] - high)
            whole = whole + factor
            summed = summed + factor * arecv[p, rows, :].astype(jnp.float32)
        for o in range(2):
            pair_own[o, layer * OWN : (layer + 1) * OWN, :] = summed[o * OWN : (o + 1) * OWN]
        notes = jnp.where(lane32 == 2 * layer, high, notes)
        notes = jnp.where(lane32 == 2 * layer + 1, whole, notes)
    loop(1, RANKS, lambda k: rank_arrived(*project, k))
    projected = precv[0]
    for p in range(1, RANKS):
        projected = projected + precv[p]
    for o in range(2):
        pair_own[o, 2 * OWN : 3 * OWN, :] = notes[o * OWN : (o + 1) * OWN]
        pair_own[o, 3 * OWN :, :] = projected

    pair = copy_of(pair_own.at[1 - xl], pair_in, pair_sem.at[0], pair_sem.at[1], to_pair)
    pair.start()
    pl.when(high_rank)(last_pieces)
    pair.wait_recv()
    joined = []
    for layer in range(LAYERS):
        sums, highs, wholes = [], [], []
        for half in (pair_own.at[xl], pair_in):
            sums.append(half[layer * OWN : (layer + 1) * OWN, :])
            highs.append(half[2 * OWN : 3 * OWN, 2 * layer : 2 * layer + 1])
            wholes.append(half[2 * OWN : 3 * OWN, 2 * layer + 1 : 2 * layer + 2])
        high = jnp.maximum(*highs)
        factors = [jnp.exp2(h - high) for h in highs]
        whole = wholes[0] * factors[0] + wholes[1] * factors[1]
        summed = sums[0] * factors[0] + sums[1] * factors[1]
        joined.append((high, whole, summed))
    projected = (pair_own[xl, 3 * OWN :, :] + pair_in[3 * OWN :, :]) * (ROWS * PEERS) ** -0.5

    def biased(kind):
        lines = [
            jnp.broadcast_to(bias[layer : layer + 1, kind * HD : (kind + 1) * HD], (8, HD))
            for layer in range(LAYERS)
        ]
        return projected[kind * 8 : kind * 8 + 8] + jnp.where(turn_row < STEPS, lines[0], lines[1])

    key = biased(0)
    key = (key * cosine + pltpu.roll(key, HD // 2, 1) * sine).astype(jnp.bfloat16)
    value = biased(1).astype(jnp.bfloat16)
    row = lax.broadcasted_iota(jnp.int32, (OWN, LAYERS * STEPS), 0)
    col = lax.broadcasted_iota(jnp.int32, (OWN, LAYERS * STEPS), 1)
    for layer in range(LAYERS):
        query = qp[layer, pl.ds(pl.multiple_of(t * OWN, OWN), OWN), :]
        s = lax.dot_general(
            query, key, (((1,), (1,)), ((), ())), preferred_element_type=jnp.float32
        )
        allowed = (col // STEPS == layer) & (col % STEPS <= row // STEPS)
        s = jnp.where(allowed, s * EXP_SCALE, NEG)
        high, whole, summed = joined[layer]
        top_all = jnp.maximum(high, jnp.max(s, axis=1, keepdims=True))
        e = jnp.exp2(s - top_all)
        factor = jnp.exp2(high - top_all)
        whole = whole * factor + jnp.sum(e, axis=1, keepdims=True)
        summed = summed * factor + jnp.dot(
            e.astype(jnp.bfloat16), value, preferred_element_type=jnp.float32
        )
        result = (summed / whole).astype(jnp.bfloat16)
        for step in range(STEPS):
            out_ref[layer, 0, step] = result[step * 4 : step * 4 + 4]

    for i, slot in enumerate([me] + others):
        for layer in range(LAYERS):
            sib_copy(i, flip(slot), layer).wait_recv()
            sib_copy(i, slot, layer).wait_send()

    def sent(j):
        for copy in own_copies(j) + cross_copies(j) + [y2_copy(j), far_copy(j)]:
            copy.wait_send()

    loop(0, CHUNKS, sent)
    loop(1, CHIPS, lambda k: h_copy(k).wait_send())
    h_sib(c).wait_send()
    loop(1, SLOTS, lambda k: part_copy(k).wait_send())
    for layer in range(LAYERS):
        loop(1, RANKS, lambda k, layer=layer: rank_copy(*attention[layer], k).wait_send())
    loop(1, RANKS, lambda k: rank_copy(*project, k).wait_send())
    pair.wait_send()


def place_kernel(map_ref, gat, part, out_hbm, part_out, sem, part_sem):
    last = pltpu.make_async_copy(part, part_out, part_sem)
    last.start()
    copies = []
    for group in range(SLOTS):
        for layer in range(LAYERS):
            copy = pltpu.make_async_copy(
                gat.at[map_ref[group], layer],
                out_hbm.at[layer, :, pl.ds(group * HD, HD)],
                sem.at[group, layer],
            )
            copy.start()
            copies.append(copy)
    for copy in copies:
        copy.wait()
    last.wait()


def on_device(
    hidden, resident, delta_codes, scales, owner_map, key_value_bias, queries, key_cache,
    value_cache, lengths,
):
    inverse = (ROPE_BASE ** (-2.0 * np.arange(HD // 2) / HD)).astype(np.float32)
    inverse = jnp.asarray(np.concatenate([inverse, inverse])[None, :])
    smem = pl.BlockSpec(memory_space=pltpu.SMEM)
    vmem = pl.BlockSpec(memory_space=pltpu.VMEM)
    hbm = pl.BlockSpec(memory_space=pltpu.HBM)
    anywhere = pl.BlockSpec(memory_space=pl.ANY)
    dma = pltpu.SemaphoreType.DMA
    f32, bf16 = jnp.float32, jnp.bfloat16
    part_shape = (LAYERS, 1, STEPS, HEADS // PEERS, HD)
    arrays = (
        owner_map, lengths, hidden, resident, delta_codes,
        scales.reshape(LAYERS, ROWS), key_value_bias, inverse,
        queries.reshape(LAYERS, QROWS, HD),
        key_cache.reshape(LAYERS, COLS, HD), value_cache.reshape(LAYERS, COLS, HD),
    )
    gathered, part, chosen = pl.pallas_call(
        gather_kernel,
        out_shape=(
            pltpu.VMEM((SLOTS, LAYERS, ROWS, HD), bf16),
            jax.ShapeDtypeStruct(part_shape, bf16),
            pltpu.SMEM((SLOTS,), jnp.int32),
        ),
        in_specs=[hbm, smem] + [hbm] * 9,
        out_specs=(vmem, vmem, smem),
        scratch_shapes=[
            pltpu.SMEM((SLOTS,), jnp.int32),
            pltpu.VMEM((LAYERS, 1, STEPS, ROWS), bf16),
            pltpu.VMEM((LAYERS, ROWS, SLOTS * HD), bf16),
            pltpu.VMEM((LAYERS, ROWS, HD), bf16),
            pltpu.VMEM((LAYERS, ROWS), bf16),
            pltpu.VMEM((LAYERS, SLOTS * HD), bf16),
            pltpu.VMEM((1, HD), f32),
            pltpu.VMEM((LAYERS, QROWS, HD), bf16),
            pltpu.VMEM((LAYERS, COLS, HD), bf16),
            pltpu.VMEM((LAYERS, COLS, HD), bf16),
            pltpu.VMEM((2, CHIPS, 16, 256), bf16),
            pltpu.VMEM((LAYERS, QROWS, HD), bf16),
            pltpu.VMEM((QROWS, COLS), f32),
            pltpu.VMEM((QROWS, HD), f32),
            pltpu.VMEM((QROWS, HD), f32),
            pltpu.VMEM((QROWS, HD), f32),
            pltpu.VMEM((QROWS, HD), f32),
            pltpu.VMEM((QROWS, HD), f32),
            pltpu.VMEM((RANKS, 5 * OWN, HD), bf16),
            pltpu.VMEM((RANKS, 5 * OWN, HD), bf16),
            pltpu.VMEM((SLOTS, LAYERS * STEPS, HD), f32),
            pltpu.VMEM((SLOTS, LAYERS * STEPS, HD), f32),
            pltpu.VMEM((RANKS, 16, HD), f32),
            pltpu.VMEM((RANKS, 16, HD), f32),
            pltpu.VMEM((2, 4 * OWN, HD), f32),
            pltpu.VMEM((4 * OWN, HD), f32),
            dma((13,)),
            dma((SLOTS, CHUNKS)),
            dma((SLOTS, LAYERS)),
            dma((3, CHUNKS)),
            dma((CHUNKS,)),
            dma((2, CHUNKS)),
            dma((CHUNKS,)),
            dma((8, LAYERS)),
            dma((CHIPS + 1,)),
            dma((CHIPS,)),
            pltpu.SemaphoreType.REGULAR,
            dma((LAYERS, RANKS)),
            dma((LAYERS, RANKS)),
            dma((SLOTS,)),
            dma((SLOTS,)),
            dma((RANKS,)),
            dma((RANKS,)),
            dma((2,)),
        ],
        compiler_params=pltpu.CompilerParams(
            collective_id=0, has_side_effects=True, vmem_limit_bytes=40 * MIB
        ),
    )(*(a if a.size == 1 else pltpu.with_memory_space_constraint(a, pltpu.HBM) for a in arrays))
    return pl.pallas_call(
        place_kernel,
        out_shape=(
            jax.ShapeDtypeStruct((LAYERS, ROWS, SLOTS * HD), bf16),
            jax.ShapeDtypeStruct(part_shape, bf16),
        ),
        in_specs=[smem, vmem, vmem],
        out_specs=(anywhere, anywhere),
        scratch_shapes=[dma((SLOTS, LAYERS)), dma(())],
        compiler_params=pltpu.CompilerParams(vmem_limit_bytes=16 * MIB),
    )(chosen, gathered, part)


def solution(mesh):
    in_specs = (
        P(None, "replica", None, "tensor"),
        P(None, "tensor", None),
        P(None, "tensor", "replica"),
        P(None, "tensor", "replica"),
        P(),
        P(),
        P(None, "replica", None, None, None),
        P(None, "replica", "tensor", None, None),
        P(None, "replica", "tensor", None, None),
        P("replica"),
    )
    out_specs = (P(None, "tensor", None), P(None, "replica", None, "tensor", None))
    return jax.shard_map(
        on_device, mesh=mesh, in_specs=in_specs, out_specs=out_specs, check_vma=False
    )
```

```python
import functools
import math

import jax
import jax.numpy as jnp
import numpy as np
from jax import lax
from jax.experimental import pallas as pl
from jax.experimental.pallas import tpu as pltpu
from jax.sharding import PartitionSpec as P

MESH = pl.DeviceIdType.MESH
ROPE_BASE = 1000000.0
MIB = 1 << 20
NEG = -1e30

LAYERS = 2
STEPS = 4
ROWS = 512
HD = 128
SLOTS = 16
PEERS = 16
RANKS = 8
HEADS = 64
KVH = 8
QROWS = STEPS * HEADS
OWN = QROWS // PEERS
SPOTS = 512
COLS = SPOTS * KVH
WIDE = 1024
CHIPS = 8
CHUNKS = 4
HALF = ROWS * LAYERS // CHUNKS
EXP_SCALE = HD**-0.5 * math.log2(math.e)


def place():
    replica = lax.axis_index("replica")
    return replica // 8, (replica // 2) % 4, replica % 2, lax.axis_index("tensor")


def slot_of(xh, y, c):
    return (xh * 4 + y) * 2 + c


def gather_kernel(
    map_hbm, len_ref, hid_hbm, res_hbm, code_hbm, scale_hbm, bias_hbm, inv_hbm, q_hbm, k_hbm, v_hbm,
    gat, out_ref, map_out,
    map_ref, hid_ref, res, code_ref, scale_ref, bias_ref, inv_ref, q_ref, kbuf, vbuf,
    hall, qp, sbuf, top, peak, total, acc, side, asend, arecv, part, proj, psend, precv, pair_own, pair_in,
    load_sem, r_sem, sib_r_sem, own_sem, y2_sem, cross_sem, far_sem, sib_sem,
    h_r_sem, h_sem, token_sem, as_sem, ar_sem, part_sem, part_r_sem, ps_sem, pr_sem, pair_sem,
):
    xh, y, c, t = place()
    me = slot_of(xh, y, c)

    pairs = [
        (map_hbm, map_ref), (hid_hbm, hid_ref), (scale_hbm, scale_ref), (code_hbm, code_ref),
    ]
    for j in range(CHUNKS):
        rows = pl.ds((j % 2) * HALF, HALF)
        pairs.append((res_hbm.at[j // 2, rows, :], res.at[j // 2, rows, :]))
    pairs += [
        (q_hbm, q_ref), (k_hbm, kbuf), (v_hbm, vbuf), (bias_hbm, bias_ref), (inv_hbm, inv_ref),
    ]
    loads = [pltpu.make_async_copy(a, b, load_sem.at[i]) for i, (a, b) in enumerate(pairs)]
    load_map, load_hid, load_scale, load_code = loads[:4]
    load_res, (load_q, load_k, load_v, load_bias, load_inv) = loads[4:8], loads[8:]
    for load in loads[:8]:
        load.start()

    def loop(low, high, body):
        def step(j, carry):
            body(j)
            return carry

        lax.fori_loop(low, high, step, 0)

    def device(x2, y2, c2):
        return (slot_of(x2, y2, c2), t)

    y_up, y_down, y_far = (y + 1) % 4, (y + 3) % 4, (y + 2) % 4
    to_up, to_down = device(xh, y_up, c), device(xh, y_down, c)
    to_x, to_sib = device(1 - xh, y, c), device(xh, y, 1 - c)

    barrier = pltpu.get_barrier_semaphore()
    chip = xh * 4 + y
    pl.semaphore_signal(barrier, inc=1, device_id=to_sib, device_id_type=MESH)

    def chip_device(k):
        return (((chip + k) % CHIPS) * 2 + c, t)

    def greet_chip(k):
        pl.semaphore_signal(barrier, inc=1, device_id=chip_device(k), device_id_type=MESH)

    loop(1, CHIPS, greet_chip)

    z, xl = t // 2, t % 2
    low, high_rank = z < RANKS // 2, z >= RANKS // 2

    def rank_device(k):
        return (me, k * 2 + xl)

    to_pair = (me, z * 2 + 1 - xl)

    def greet(k):
        pl.semaphore_signal(barrier, inc=1, device_id=rank_device(k), device_id_type=MESH)

    loop(z + 1, RANKS, greet)

    @pl.when(xl == 0)
    def _():
        pl.semaphore_signal(barrier, inc=1, device_id=to_pair, device_id_type=MESH)

    load_map.wait()
    group = jnp.int32(0)
    for g in range(SLOTS):
        group = group + jnp.where(map_ref[g] == me, g, 0)
        map_out[g] = map_ref[g]
    group_all = jnp.broadcast_to(group.astype(jnp.float32), (HD, HD)).astype(jnp.bfloat16)

    def own_block(j):
        load_res[j].wait()
        layer = j // 2
        for p in range(HALF // HD):
            rows = pl.ds((j % 2) * HALF + p * HD, HD)
            line = scale_ref[pl.ds(layer, 1), rows].astype(jnp.float32)
            column = jnp.transpose(jnp.broadcast_to(line, (HD, HD)))
            code = code_ref[layer, rows, :].astype(jnp.float32)
            base = res[layer, rows, :HD]
            for g in range(1, SLOTS):
                base = jnp.where(group_all == g, res[layer, rows, g * HD : (g + 1) * HD], base)
            base = base.astype(jnp.float32)
            gat[me, layer, rows, :] = (base + code * column).astype(jnp.bfloat16)

    load_hid.wait()
    halves = [
        hid_ref[layer, 0, :, h * 256 : (h + 1) * 256].astype(jnp.float32)
        for h in range(2)
        for layer in range(LAYERS)
    ]
    hall[c, chip] = jnp.concatenate(halves, axis=0).astype(jnp.bfloat16)

    pl.semaphore_wait(barrier, CHIPS + z + xl)

    def copy_of(src, dst, s_sem, rr_sem, target):
        return pltpu.make_async_remote_copy(
            src_ref=src, dst_ref=dst, send_sem=s_sem, recv_sem=rr_sem,
            device_id=target, device_id_type=MESH,
        )

    s_up, s_down = slot_of(xh, y_up, c), slot_of(xh, y_down, c)
    s_far, s_x = slot_of(xh, y_far, c), slot_of(1 - xh, y, c)
    x_up, x_down = slot_of(1 - xh, y_up, c), slot_of(1 - xh, y_down, c)
    x_far = slot_of(1 - xh, y_far, c)
    others = [s_up, s_down, s_x, s_far, x_up, x_down, x_far]

    def flip(slot):
        return slot + 1 - 2 * c

    def h_copy(k):
        return copy_of(
            hall.at[c, chip], hall.at[c, chip], h_sem.at[k], h_r_sem.at[chip], chip_device(k)
        )

    def h_arrived(k):
        other = (chip + k) % CHIPS
        copy_of(
            hall.at[c, other], hall.at[c, other], h_sem.at[k], h_r_sem.at[other], to_sib
        ).wait_recv()

    def h_sib(core):
        return copy_of(hall.at[core], hall.at[core], h_sem.at[0], h_r_sem.at[CHIPS], to_sib)

    def rows_of(slot, j, count):
        return gat.at[slot, j // 2, pl.ds(pl.multiple_of((j % 2) * HALF, HALF), HALF * count), :]

    def send(slot, j, sem, target):
        ref = rows_of(slot, j, 1)
        return copy_of(ref, ref, sem, r_sem.at[slot, j], target)

    def arrived(slot, j):
        send(slot, j, r_sem.at[slot, j], to_sib).wait_recv()

    def sib_copy(i, slot, layer):
        ref = gat.at[slot, layer]
        return copy_of(ref, ref, sib_sem.at[i, layer], sib_r_sem.at[slot, layer], to_sib)

    def sib_send(i, layer):
        sib_copy(i, others[i - 1] if i else me, layer).start()

    def own_copies(j):
        return [
            send(me, j, own_sem.at[0, j], to_up),
            send(me, j, own_sem.at[1, j], to_down),
            send(me, j, own_sem.at[2, j], to_x),
        ]

    def onward(j):
        up = 1 - 2 * (j % 2)
        return slot_of(xh, (y + 4 - up) % 4, c), device(xh, (y + 4 + up) % 4, c)

    def y2_copy(j):
        slot, target = onward(j)
        return send(slot, j, y2_sem.at[j], target)

    def cross_copies(j):
        return [send(s_x, j, cross_sem.at[0, j], to_up), send(s_x, j, cross_sem.at[1, j], to_down)]

    def far_copy(j):
        return send(s_far, j, far_sem.at[j], to_x)

    def y2_step(j):
        slot, _ = onward(j)
        arrived(slot, j)
        y2_copy(j).start()

    def cross_step(j):
        arrived(s_x, j)
        for copy in cross_copies(j):
            copy.start()

    def far_step(j):
        arrived(s_far, j)
        far_copy(j).start()

    loop(1, CHIPS, lambda k: h_copy(k).start())

    def own_step(j):
        for copy in own_copies(j):
            copy.start()

    load_scale.wait()
    load_code.wait()
    for j in range(CHUNKS):
        own_block(j)
        own_step(j)
        if j == 0:
            for load in loads[8:]:
                load.start()

    def answer(k):
        pl.semaphore_signal(token_sem, inc=1, device_id=rank_device(k), device_id_type=MESH)

    loop(0, z, answer)

    @pl.when(xl == 1)
    def _():
        pl.semaphore_signal(token_sem, inc=1, device_id=to_pair, device_id_type=MESH)

    load_q.wait()
    row = lax.broadcasted_iota(jnp.int32, (QROWS, QROWS), 0)
    col = lax.broadcasted_iota(jnp.int32, (QROWS, QROWS), 1)
    source = ((row // STEPS) % STEPS) * HEADS + (row // OWN) * STEPS + row % STEPS
    pick = jnp.where(col == source, 1.0, 0.0).astype(jnp.bfloat16)
    for layer in range(LAYERS):
        qp[layer] = jnp.dot(pick, q_ref[layer], preferred_element_type=jnp.float32).astype(
            jnp.bfloat16
        )
    length = len_ref[0]
    limit = (length - t * SPOTS) * KVH
    lanes = lax.broadcasted_iota(jnp.int32, (1, WIDE), 1)
    lane = lax.broadcasted_iota(jnp.int32, (QROWS, HD), 1)
    valid = lane % KVH == lax.broadcasted_iota(jnp.int32, (QROWS, HD), 0) // (QROWS // KVH)

    def scores(layer):
        top[...] = jnp.full((QROWS, HD), NEG, jnp.float32)
        for n in range(COLS // WIDE):
            first = n * WIDE
            s = lax.dot_general(
                qp[layer], kbuf[layer, first : first + WIDE, :], (((1,), (1,)), ((), ())),
                preferred_element_type=jnp.float32,
            )
            s = s + jnp.where(lanes + first < limit, 0.0, NEG)
            sbuf[:, first : first + WIDE] = s
            high = top[...]
            for i in range(WIDE // HD):
                high = jnp.maximum(high, s[:, i * HD : (i + 1) * HD])
            top[...] = high
        high = jnp.max(jnp.where(valid, top[...], NEG), axis=1, keepdims=True)
        peak[...] = jnp.broadcast_to(high, (QROWS, HD))
        top[...] = jnp.where(valid, high, -NEG)

    def values(layer):
        total[...] = jnp.zeros((QROWS, HD), jnp.float32)
        acc[...] = jnp.zeros((QROWS, HD), jnp.float32)
        for n in range(COLS // WIDE):
            first = n * WIDE
            high = top[...]
            added = total[...]
            pieces = []
            for i in range(WIDE // HD):
                e = jnp.exp2((sbuf[:, first + i * HD : first + (i + 1) * HD] - high) * EXP_SCALE)
                added = added + e
                pieces.append(e.astype(jnp.bfloat16))
            total[...] = added
            acc[...] += jnp.dot(
                jnp.concatenate(pieces, axis=1), vbuf[layer, first : first + WIDE, :],
                preferred_element_type=jnp.float32,
            )
        whole = jnp.broadcast_to(jnp.sum(total[...], axis=1, keepdims=True), (QROWS, HD))
        asend[:, layer * 2 * OWN : (layer + 1) * 2 * OWN, :] = (
            (acc[...] / whole).astype(jnp.bfloat16).reshape(RANKS, 2 * OWN, HD)
        )
        rest = peak[...] * EXP_SCALE + jnp.log(whole) * math.log2(math.e)
        kept = side[...] if layer else jnp.zeros((QROWS, HD), jnp.float32)
        for i in range(3):
            term = rest.astype(jnp.bfloat16).astype(jnp.float32)
            rest = rest - term
            kept = jnp.where(lane == 3 * layer + i, term, kept)
        side[...] = kept

    def rank_copy(src, dst, s_sem, rr_sem, k):
        target = (z + k) % RANKS
        return copy_of(
            src(target), dst(z), s_sem.at[target], rr_sem.at[z], rank_device(target)
        )

    def rank_arrived(src, dst, s_sem, rr_sem, k):
        other = (z + k) % RANKS
        copy_of(
            src(other), dst(other), s_sem.at[other], rr_sem.at[other], rank_device(other)
        ).wait_recv()

    def run_of(ref, layer):
        return lambda rank: ref.at[rank, 0:32] if layer == 0 else ref.at[rank, 32:80]

    attention = [
        (run_of(asend, layer), run_of(arecv, layer), as_sem.at[layer], ar_sem.at[layer])
        for layer in range(LAYERS)
    ]
    project = (lambda rank: psend.at[rank], lambda rank: precv.at[rank], ps_sem, pr_sem)

    def answered():
        answers = (RANKS - 1 - z) + (1 - xl)
        pl.when(answers > 0)(lambda: pl.semaphore_wait(token_sem, answers))

    def send_attention(layer):
        loop(1, RANKS, lambda k: rank_copy(*attention[layer], k).start())

    def send_project():
        loop(1, RANKS, lambda k: rank_copy(*project, k).start())

    load_k.wait()
    scores(0)
    loop(1, CHIPS, h_arrived)
    h_sib(c).start()
    load_v.wait()
    values(0)

    @pl.when(high_rank)
    def _():
        answered()
        send_attention(0)

    for layer in range(LAYERS):
        sib_send(0, layer)
    pl.when(low)(lambda: loop(0, 2, y2_step))
    h_sib(1 - c).wait_recv()

    rows8 = lax.broadcasted_iota(jnp.int32, (SLOTS, LAYERS * STEPS, HD), 1)
    product = []
    for layer in range(LAYERS):
        halves = [
            jnp.dot(
                hall[...].reshape(SLOTS * 16, 256), gat[me, layer, h * 256 : (h + 1) * 256, :],
                preferred_element_type=jnp.float32,
            ).reshape(SLOTS, 16, HD)
            for h in range(2)
        ]
        product.append(halves[0][:, :8] + halves[1][:, 8:])
    part[...] = jnp.where(rows8 < STEPS, product[0], product[1])

    def part_copy(k):
        target = (me + k) % SLOTS
        return copy_of(
            part.at[(target % 2) * CHIPS + target // 2], proj.at[me],
            part_sem.at[target], part_r_sem.at[me], (target, t),
        )

    def part_arrived(k):
        other = (me + k) % SLOTS
        copy_of(
            part.at[other], proj.at[other], part_sem.at[other], part_r_sem.at[other], to_sib
        ).wait_recv()

    loop(1, SLOTS, lambda k: part_copy(k).start())
    proj[me] = part[c * CHIPS + chip]

    scores(1)
    @pl.when(low)
    def _():
        loop(2, CHUNKS, y2_step)
        loop(0, 2, cross_step)

    pl.when(high_rank)(lambda: loop(0, 2, y2_step))
    values(1)
    notes = side[...].reshape(RANKS, 2 * OWN, HD)
    second = pltpu.roll(notes[:, OWN:].reshape(RANKS * OWN, HD), HD // 2, 1)
    lane3 = lax.broadcasted_iota(jnp.int32, (RANKS, OWN, HD), 2)
    notes = jnp.where(lane3 < HD // 2, notes[:, :OWN], second.reshape(RANKS, OWN, HD))
    asend[:, 4 * OWN :, :] = notes.astype(jnp.bfloat16)
    @pl.when(high_rank)
    def _():
        send_attention(1)
        loop(2, CHUNKS, y2_step)
        loop(0, 2, cross_step)


    def opposite_step(j):
        arrived(slot_of(xh, (y + 4 + 1 - 2 * (j % 2)) % 4, c), j)

    def far_steps():
        loop(2, CHUNKS, far_step)
        loop(0, CHUNKS, opposite_step)
        for layer in range(LAYERS):
            for i in range(4):
                sib_send(i + 1, layer)

    @pl.when(low)
    def _():
        loop(2, CHUNKS, cross_step)
        loop(0, 2, far_step)
        far_steps()
        answered()
        send_attention(0)
        send_attention(1)

    loop(1, SLOTS, part_arrived)
    for g in range(SLOTS):
        slot_all = jnp.broadcast_to(map_ref[g], (LAYERS * STEPS, HD))
        line = proj[0]
        for slot in range(1, SLOTS):
            line = jnp.where(slot_all == slot, proj[slot], line)
        psend[g // 2, (g % 2) * 8 : (g % 2) * 8 + 8, :] = line
    precv[z] = psend[z]
    arecv[z] = asend[z]

    send_project()

    @pl.when(high_rank)
    def _():
        loop(2, CHUNKS, cross_step)
        loop(0, 2, far_step)
        far_steps()

    load_bias.wait()
    load_inv.wait()
    turn_row = lax.broadcasted_iota(jnp.int32, (LAYERS * STEPS, HD), 0)
    turn_lane = lax.broadcasted_iota(jnp.int32, (LAYERS * STEPS, HD), 1)
    angle = (length + turn_row % STEPS).astype(jnp.float32) * inv_ref[...]
    cosine = jnp.cos(angle)
    sine = jnp.where(turn_lane < HD // 2, -1.0, 1.0) * jnp.sin(angle)
    head = t // 2
    bias = bias_ref[:, pl.ds(pl.multiple_of(head * 2 * HD, 2 * HD), 2 * HD)].astype(jnp.float32)

    def last_pieces(layer):
        for i, slot in ((5, x_up), (6, x_down), (7, x_far)):
            loop(2 * layer, 2 * layer + 2, lambda j, slot=slot: arrived(slot, j))
            sib_send(i, layer)

    last_pieces(0)
    pl.when(z < 2)(lambda: last_pieces(1))

    for layer in range(LAYERS):
        loop(1, RANKS, lambda k, layer=layer: rank_arrived(*attention[layer], k))
    lane32 = lax.broadcasted_iota(jnp.int32, (2 * OWN, HD), 1)
    sides = [arecv[p, 4 * OWN :, :].astype(jnp.float32) for p in range(RANKS)]
    notes = jnp.zeros((2 * OWN, HD), jnp.float32)
    for layer in range(LAYERS):
        logs = []
        for x in sides:
            firsts = (3 * layer, 3 * layer + HD // 2)
            columns = [sum(x[:, n + i : n + i + 1] for i in range(3)) for n in firsts]
            logs.append(jnp.concatenate(columns, axis=0))
        high = functools.reduce(jnp.maximum, logs)
        whole = jnp.zeros((2 * OWN, 1), jnp.float32)
        summed = jnp.zeros((2 * OWN, HD), jnp.float32)
        rows = slice(layer * 2 * OWN, (layer + 1) * 2 * OWN)
        for p in range(RANKS):
            factor = jnp.exp2(logs[p] - high)
            whole = whole + factor
            summed = summed + factor * arecv[p, rows, :].astype(jnp.float32)
        for o in range(2):
            pair_own[o, layer * OWN : (layer + 1) * OWN, :] = summed[o * OWN : (o + 1) * OWN]
        notes = jnp.where(lane32 == 2 * layer, high, notes)
        notes = jnp.where(lane32 == 2 * layer + 1, whole, notes)
    for o in range(2):
        pair_own[o, 2 * OWN : 3 * OWN, :] = notes[o * OWN : (o + 1) * OWN]

    def pair_copy(n, low_row, count):
        rows = pl.ds(low_row, count)
        return copy_of(
            pair_own.at[1 - xl, rows, :], pair_in.at[rows, :],
            pair_sem.at[n, 0], pair_sem.at[n, 1], to_pair,
        )

    pair = [pair_copy(0, 0, 3 * OWN), pair_copy(1, 3 * OWN, OWN)]
    pair[0].start()
    loop(1, RANKS, lambda k: rank_arrived(*project, k))
    projected = precv[0]
    for p in range(1, RANKS):
        projected = projected + precv[p]
    for o in range(2):
        pair_own[o, 3 * OWN :, :] = projected
    pair[1].start()
    pl.when(z >= 2)(lambda: last_pieces(1))
    pair[0].wait_recv()
    joined = []
    for layer in range(LAYERS):
        sums, highs, wholes = [], [], []
        for half in (pair_own.at[xl], pair_in):
            sums.append(half[layer * OWN : (layer + 1) * OWN, :])
            highs.append(half[2 * OWN : 3 * OWN, 2 * layer : 2 * layer + 1])
            wholes.append(half[2 * OWN : 3 * OWN, 2 * layer + 1 : 2 * layer + 2])
        high = jnp.maximum(*highs)
        factors = [jnp.exp2(h - high) for h in highs]
        whole = wholes[0] * factors[0] + wholes[1] * factors[1]
        summed = sums[0] * factors[0] + sums[1] * factors[1]
        joined.append((high, whole, summed))
    pair[1].wait_recv()
    projected = (pair_own[xl, 3 * OWN :, :] + pair_in[3 * OWN :, :]) * (ROWS * PEERS) ** -0.5

    def biased(kind):
        lines = [
            jnp.broadcast_to(bias[layer : layer + 1, kind * HD : (kind + 1) * HD], (8, HD))
            for layer in range(LAYERS)
        ]
        return projected[kind * 8 : kind * 8 + 8] + jnp.where(turn_row < STEPS, lines[0], lines[1])

    key = biased(0)
    key = (key * cosine + pltpu.roll(key, HD // 2, 1) * sine).astype(jnp.bfloat16)
    value = biased(1).astype(jnp.bfloat16)
    row = lax.broadcasted_iota(jnp.int32, (OWN, LAYERS * STEPS), 0)
    col = lax.broadcasted_iota(jnp.int32, (OWN, LAYERS * STEPS), 1)
    for layer in range(LAYERS):
        query = qp[layer, pl.ds(pl.multiple_of(t * OWN, OWN), OWN), :]
        s = lax.dot_general(
            query, key, (((1,), (1,)), ((), ())), preferred_element_type=jnp.float32
        )
        allowed = (col // STEPS == layer) & (col % STEPS <= row // STEPS)
        s = jnp.where(allowed, s * EXP_SCALE, NEG)
        high, whole, summed = joined[layer]
        top_all = jnp.maximum(high, jnp.max(s, axis=1, keepdims=True))
        e = jnp.exp2(s - top_all)
        factor = jnp.exp2(high - top_all)
        whole = whole * factor + jnp.sum(e, axis=1, keepdims=True)
        summed = summed * factor + jnp.dot(
            e.astype(jnp.bfloat16), value, preferred_element_type=jnp.float32
        )
        result = (summed / whole).astype(jnp.bfloat16)
        for step in range(STEPS):
            out_ref[layer, 0, step] = result[step * 4 : step * 4 + 4]

    for i, slot in enumerate([me] + others):
        for layer in range(LAYERS):
            sib_copy(i, flip(slot), layer).wait_recv()
            sib_copy(i, slot, layer).wait_send()

    def sent(j):
        for copy in own_copies(j) + cross_copies(j) + [y2_copy(j), far_copy(j)]:
            copy.wait_send()

    loop(0, CHUNKS, sent)
    loop(1, CHIPS, lambda k: h_copy(k).wait_send())
    h_sib(c).wait_send()
    loop(1, SLOTS, lambda k: part_copy(k).wait_send())
    for layer in range(LAYERS):
        loop(1, RANKS, lambda k, layer=layer: rank_copy(*attention[layer], k).wait_send())
    loop(1, RANKS, lambda k: rank_copy(*project, k).wait_send())
    for copy in pair:
        copy.wait_send()


def place_kernel(map_ref, gat, part, out_hbm, part_out, sem, part_sem):
    last = pltpu.make_async_copy(part, part_out, part_sem)
    last.start()
    copies = []
    for group in range(SLOTS):
        for layer in range(LAYERS):
            copy = pltpu.make_async_copy(
                gat.at[map_ref[group], layer],
                out_hbm.at[layer, :, pl.ds(group * HD, HD)],
                sem.at[group, layer],
            )
            copy.start()
            copies.append(copy)
    for copy in copies:
        copy.wait()
    last.wait()


def on_device(
    hidden, resident, delta_codes, scales, owner_map, key_value_bias, queries, key_cache,
    value_cache, lengths,
):
    inverse = (ROPE_BASE ** (-2.0 * np.arange(HD // 2) / HD)).astype(np.float32)
    inverse = jnp.asarray(np.concatenate([inverse, inverse])[None, :])
    smem = pl.BlockSpec(memory_space=pltpu.SMEM)
    vmem = pl.BlockSpec(memory_space=pltpu.VMEM)
    hbm = pl.BlockSpec(memory_space=pltpu.HBM)
    anywhere = pl.BlockSpec(memory_space=pl.ANY)
    dma = pltpu.SemaphoreType.DMA
    f32, bf16 = jnp.float32, jnp.bfloat16
    part_shape = (LAYERS, 1, STEPS, HEADS // PEERS, HD)
    arrays = (
        owner_map, lengths, hidden, resident, delta_codes,
        scales.reshape(LAYERS, ROWS), key_value_bias, inverse,
        queries.reshape(LAYERS, QROWS, HD),
        key_cache.reshape(LAYERS, COLS, HD), value_cache.reshape(LAYERS, COLS, HD),
    )
    gathered, part, chosen = pl.pallas_call(
        gather_kernel,
        out_shape=(
            pltpu.VMEM((SLOTS, LAYERS, ROWS, HD), bf16),
            jax.ShapeDtypeStruct(part_shape, bf16),
            pltpu.SMEM((SLOTS,), jnp.int32),
        ),
        in_specs=[hbm, smem] + [hbm] * 9,
        out_specs=(vmem, vmem, smem),
        scratch_shapes=[
            pltpu.SMEM((SLOTS,), jnp.int32),
            pltpu.VMEM((LAYERS, 1, STEPS, ROWS), bf16),
            pltpu.VMEM((LAYERS, ROWS, SLOTS * HD), bf16),
            pltpu.VMEM((LAYERS, ROWS, HD), bf16),
            pltpu.VMEM((LAYERS, ROWS), bf16),
            pltpu.VMEM((LAYERS, SLOTS * HD), bf16),
            pltpu.VMEM((1, HD), f32),
            pltpu.VMEM((LAYERS, QROWS, HD), bf16),
            pltpu.VMEM((LAYERS, COLS, HD), bf16),
            pltpu.VMEM((LAYERS, COLS, HD), bf16),
            pltpu.VMEM((2, CHIPS, 16, 256), bf16),
            pltpu.VMEM((LAYERS, QROWS, HD), bf16),
            pltpu.VMEM((QROWS, COLS), f32),
            pltpu.VMEM((QROWS, HD), f32),
            pltpu.VMEM((QROWS, HD), f32),
            pltpu.VMEM((QROWS, HD), f32),
            pltpu.VMEM((QROWS, HD), f32),
            pltpu.VMEM((QROWS, HD), f32),
            pltpu.VMEM((RANKS, 5 * OWN, HD), bf16),
            pltpu.VMEM((RANKS, 5 * OWN, HD), bf16),
            pltpu.VMEM((SLOTS, LAYERS * STEPS, HD), f32),
            pltpu.VMEM((SLOTS, LAYERS * STEPS, HD), f32),
            pltpu.VMEM((RANKS, 16, HD), f32),
            pltpu.VMEM((RANKS, 16, HD), f32),
            pltpu.VMEM((2, 4 * OWN, HD), f32),
            pltpu.VMEM((4 * OWN, HD), f32),
            dma((13,)),
            dma((SLOTS, CHUNKS)),
            dma((SLOTS, LAYERS)),
            dma((3, CHUNKS)),
            dma((CHUNKS,)),
            dma((2, CHUNKS)),
            dma((CHUNKS,)),
            dma((8, LAYERS)),
            dma((CHIPS + 1,)),
            dma((CHIPS,)),
            pltpu.SemaphoreType.REGULAR,
            dma((LAYERS, RANKS)),
            dma((LAYERS, RANKS)),
            dma((SLOTS,)),
            dma((SLOTS,)),
            dma((RANKS,)),
            dma((RANKS,)),
            dma((2, 2)),
        ],
        compiler_params=pltpu.CompilerParams(
            collective_id=0, has_side_effects=True, vmem_limit_bytes=40 * MIB
        ),
    )(*(a if a.size == 1 else pltpu.with_memory_space_constraint(a, pltpu.HBM) for a in arrays))
    return pl.pallas_call(
        place_kernel,
        out_shape=(
            jax.ShapeDtypeStruct((LAYERS, ROWS, SLOTS * HD), bf16),
            jax.ShapeDtypeStruct(part_shape, bf16),
        ),
        in_specs=[smem, vmem, vmem],
        out_specs=(anywhere, anywhere),
        scratch_shapes=[dma((SLOTS, LAYERS)), dma(())],
        compiler_params=pltpu.CompilerParams(vmem_limit_bytes=16 * MIB),
    )(chosen, gathered, part)


def solution(mesh):
    in_specs = (
        P(None, "replica", None, "tensor"),
        P(None, "tensor", None),
        P(None, "tensor", "replica"),
        P(None, "tensor", "replica"),
        P(),
        P(),
        P(None, "replica", None, None, None),
        P(None, "replica", "tensor", None, None),
        P(None, "replica", "tensor", None, None),
        P("replica"),
    )
    out_specs = (P(None, "tensor", None), P(None, "replica", None, "tensor", None))
    return jax.shard_map(
        on_device, mesh=mesh, in_specs=in_specs, out_specs=out_specs, check_vma=False
    )
```

```python
import functools
import math

import jax
import jax.numpy as jnp
import numpy as np
from jax import lax
from jax.experimental import pallas as pl
from jax.experimental.pallas import tpu as pltpu
from jax.sharding import PartitionSpec as P

MESH = pl.DeviceIdType.MESH
ROPE_BASE = 1000000.0
MIB = 1 << 20
NEG = -1e30

LAYERS = 2
STEPS = 4
ROWS = 512
HD = 128
SLOTS = 16
PEERS = 16
RANKS = 8
HEADS = 64
KVH = 8
QROWS = STEPS * HEADS
OWN = QROWS // PEERS
SPOTS = 512
COLS = SPOTS * KVH
WIDE = 1024
CHIPS = 8
CHUNKS = 4
HALF = ROWS * LAYERS // CHUNKS
EXP_SCALE = HD**-0.5 * math.log2(math.e)


def place():
    replica = lax.axis_index("replica")
    return replica // 8, (replica // 2) % 4, replica % 2, lax.axis_index("tensor")


def slot_of(xh, y, c):
    return (xh * 4 + y) * 2 + c


def gather_kernel(
    map_hbm, len_ref, hid_hbm, res_hbm, code_hbm, scale_hbm, bias_hbm, inv_hbm, q_hbm, k_hbm, v_hbm,
    gat, out_ref, map_out,
    map_ref, hid_ref, res, code_ref, scale_ref, bias_ref, inv_ref, q_ref, kbuf, vbuf,
    hall, qp, sbuf, top, peak, total, acc, side, asend, arecv, part, proj, psend, precv, pair_own, pair_in,
    load_sem, r_sem, sib_r_sem, own_sem, y2_sem, cross_sem, far_sem, sib_sem,
    h_r_sem, h_sem, token_sem, as_sem, ar_sem, part_sem, part_r_sem, ps_sem, pr_sem, pair_sem,
):
    xh, y, c, t = place()
    me = slot_of(xh, y, c)

    pairs = [
        (map_hbm, map_ref), (hid_hbm, hid_ref), (scale_hbm, scale_ref), (code_hbm, code_ref),
    ]
    for j in range(CHUNKS):
        rows = pl.ds((j % 2) * HALF, HALF)
        pairs.append((res_hbm.at[j // 2, rows, :], res.at[j // 2, rows, :]))
    pairs += [
        (q_hbm, q_ref), (k_hbm, kbuf), (v_hbm, vbuf), (bias_hbm, bias_ref), (inv_hbm, inv_ref),
    ]
    loads = [pltpu.make_async_copy(a, b, load_sem.at[i]) for i, (a, b) in enumerate(pairs)]
    load_map, load_hid, load_scale, load_code = loads[:4]
    load_res, (load_q, load_k, load_v, load_bias, load_inv) = loads[4:8], loads[8:]
    for load in loads[:8]:
        load.start()

    def loop(low, high, body):
        def step(j, carry):
            body(j)
            return carry

        lax.fori_loop(low, high, step, 0)

    def device(x2, y2, c2):
        return (slot_of(x2, y2, c2), t)

    y_up, y_down, y_far = (y + 1) % 4, (y + 3) % 4, (y + 2) % 4
    to_up, to_down = device(xh, y_up, c), device(xh, y_down, c)
    to_x, to_sib = device(1 - xh, y, c), device(xh, y, 1 - c)

    barrier = pltpu.get_barrier_semaphore()
    chip = xh * 4 + y
    pl.semaphore_signal(barrier, inc=1, device_id=to_sib, device_id_type=MESH)

    def chip_device(k):
        return (((chip + k) % CHIPS) * 2 + c, t)

    def greet_chip(k):
        pl.semaphore_signal(barrier, inc=1, device_id=chip_device(k), device_id_type=MESH)

    loop(1, CHIPS, greet_chip)

    z, xl = t // 2, t % 2
    low, high_rank = z < RANKS // 2, z >= RANKS // 2

    def rank_device(k):
        return (me, k * 2 + xl)

    to_pair = (me, z * 2 + 1 - xl)

    def greet(k):
        pl.semaphore_signal(barrier, inc=1, device_id=rank_device(k), device_id_type=MESH)

    loop(z + 1, RANKS, greet)

    @pl.when(xl == 0)
    def _():
        pl.semaphore_signal(barrier, inc=1, device_id=to_pair, device_id_type=MESH)

    load_map.wait()
    group = jnp.int32(0)
    for g in range(SLOTS):
        group = group + jnp.where(map_ref[g] == me, g, 0)
        map_out[g] = map_ref[g]
    group_all = jnp.broadcast_to(group.astype(jnp.float32), (HD, HD)).astype(jnp.bfloat16)

    def own_block(j):
        load_res[j].wait()
        layer = j // 2
        for p in range(HALF // HD):
            rows = pl.ds((j % 2) * HALF + p * HD, HD)
            line = scale_ref[pl.ds(layer, 1), rows].astype(jnp.float32)
            column = jnp.transpose(jnp.broadcast_to(line, (HD, HD)))
            code = code_ref[layer, rows, :].astype(jnp.float32)
            base = res[layer, rows, :HD]
            for g in range(1, SLOTS):
                base = jnp.where(group_all == g, res[layer, rows, g * HD : (g + 1) * HD], base)
            base = base.astype(jnp.float32)
            gat[me, layer, rows, :] = (base + code * column).astype(jnp.bfloat16)

    load_hid.wait()
    halves = [
        hid_ref[layer, 0, :, h * 256 : (h + 1) * 256].astype(jnp.float32)
        for h in range(2)
        for layer in range(LAYERS)
    ]
    hall[c, chip] = jnp.concatenate(halves, axis=0).astype(jnp.bfloat16)

    pl.semaphore_wait(barrier, CHIPS + z + xl)

    def copy_of(src, dst, s_sem, rr_sem, target):
        return pltpu.make_async_remote_copy(
            src_ref=src, dst_ref=dst, send_sem=s_sem, recv_sem=rr_sem,
            device_id=target, device_id_type=MESH,
        )

    s_up, s_down = slot_of(xh, y_up, c), slot_of(xh, y_down, c)
    s_far, s_x = slot_of(xh, y_far, c), slot_of(1 - xh, y, c)
    x_up, x_down = slot_of(1 - xh, y_up, c), slot_of(1 - xh, y_down, c)
    x_far = slot_of(1 - xh, y_far, c)
    others = [s_up, s_down, s_x, s_far, x_up, x_down, x_far]

    def flip(slot):
        return slot + 1 - 2 * c

    def h_copy(k):
        return copy_of(
            hall.at[c, chip], hall.at[c, chip], h_sem.at[k], h_r_sem.at[chip], chip_device(k)
        )

    def h_arrived(k):
        other = (chip + k) % CHIPS
        copy_of(
            hall.at[c, other], hall.at[c, other], h_sem.at[k], h_r_sem.at[other], to_sib
        ).wait_recv()

    def h_sib(core):
        return copy_of(hall.at[core], hall.at[core], h_sem.at[0], h_r_sem.at[CHIPS], to_sib)

    def rows_of(slot, j, count):
        return gat.at[slot, j // 2, pl.ds(pl.multiple_of((j % 2) * HALF, HALF), HALF * count), :]

    def send(slot, j, sem, target):
        ref = rows_of(slot, j, 1)
        return copy_of(ref, ref, sem, r_sem.at[slot, j], target)

    def arrived(slot, j):
        send(slot, j, r_sem.at[slot, j], to_sib).wait_recv()

    def sib_copy(i, slot, layer):
        ref = gat.at[slot, layer]
        return copy_of(ref, ref, sib_sem.at[i, layer], sib_r_sem.at[slot, layer], to_sib)

    def sib_send(i, layer):
        sib_copy(i, others[i - 1] if i else me, layer).start()

    def own_copies(j):
        return [
            send(me, j, own_sem.at[0, j], to_up),
            send(me, j, own_sem.at[1, j], to_down),
            send(me, j, own_sem.at[2, j], to_x),
        ]

    def onward(j):
        up = 1 - 2 * (j % 2)
        return slot_of(xh, (y + 4 - up) % 4, c), device(xh, (y + 4 + up) % 4, c)

    def y2_copy(j):
        slot, target = onward(j)
        return send(slot, j, y2_sem.at[j], target)

    def cross_copies(j):
        return [send(s_x, j, cross_sem.at[0, j], to_up), send(s_x, j, cross_sem.at[1, j], to_down)]

    def far_copy(j):
        return send(s_far, j, far_sem.at[j], to_x)

    def y2_step(j):
        slot, _ = onward(j)
        arrived(slot, j)
        y2_copy(j).start()

    def cross_step(j):
        arrived(s_x, j)
        for copy in cross_copies(j):
            copy.start()

    def far_step(j):
        arrived(s_far, j)
        far_copy(j).start()

    loop(1, CHIPS, lambda k: h_copy(k).start())

    def own_step(j):
        for copy in own_copies(j):
            copy.start()

    load_scale.wait()
    load_code.wait()
    for j in range(CHUNKS):
        own_block(j)
        own_step(j)
        if j == 0:
            for load in loads[8:]:
                load.start()

    def answer(k):
        pl.semaphore_signal(token_sem, inc=1, device_id=rank_device(k), device_id_type=MESH)

    loop(0, z, answer)

    @pl.when(xl == 1)
    def _():
        pl.semaphore_signal(token_sem, inc=1, device_id=to_pair, device_id_type=MESH)

    load_q.wait()
    row = lax.broadcasted_iota(jnp.int32, (QROWS, QROWS), 0)
    col = lax.broadcasted_iota(jnp.int32, (QROWS, QROWS), 1)
    source = ((row // STEPS) % STEPS) * HEADS + (row // OWN) * STEPS + row % STEPS
    pick = jnp.where(col == source, 1.0, 0.0).astype(jnp.bfloat16)
    for layer in range(LAYERS):
        qp[layer] = jnp.dot(pick, q_ref[layer], preferred_element_type=jnp.float32).astype(
            jnp.bfloat16
        )
    length = len_ref[0]
    limit = (length - t * SPOTS) * KVH
    lanes = lax.broadcasted_iota(jnp.int32, (1, WIDE), 1)
    lane = lax.broadcasted_iota(jnp.int32, (QROWS, HD), 1)
    valid = lane % KVH == lax.broadcasted_iota(jnp.int32, (QROWS, HD), 0) // (QROWS // KVH)

    def scores(layer):
        top[...] = jnp.full((QROWS, HD), NEG, jnp.float32)
        for n in range(COLS // WIDE):
            first = n * WIDE
            s = lax.dot_general(
                qp[layer], kbuf[layer, first : first + WIDE, :], (((1,), (1,)), ((), ())),
                preferred_element_type=jnp.float32,
            )
            s = s + jnp.where(lanes + first < limit, 0.0, NEG)
            sbuf[:, first : first + WIDE] = s
            high = top[...]
            for i in range(WIDE // HD):
                high = jnp.maximum(high, s[:, i * HD : (i + 1) * HD])
            top[...] = high
        high = jnp.max(jnp.where(valid, top[...], NEG), axis=1, keepdims=True)
        peak[...] = jnp.broadcast_to(high, (QROWS, HD))
        top[...] = jnp.where(valid, high, -NEG)

    def values(layer):
        total[...] = jnp.zeros((QROWS, HD), jnp.float32)
        acc[...] = jnp.zeros((QROWS, HD), jnp.float32)
        for n in range(COLS // WIDE):
            first = n * WIDE
            high = top[...]
            added = total[...]
            pieces = []
            for i in range(WIDE // HD):
                e = jnp.exp2((sbuf[:, first + i * HD : first + (i + 1) * HD] - high) * EXP_SCALE)
                added = added + e
                pieces.append(e.astype(jnp.bfloat16))
            total[...] = added
            acc[...] += jnp.dot(
                jnp.concatenate(pieces, axis=1), vbuf[layer, first : first + WIDE, :],
                preferred_element_type=jnp.float32,
            )
        whole = jnp.broadcast_to(jnp.sum(total[...], axis=1, keepdims=True), (QROWS, HD))
        asend[:, layer * 2 * OWN : (layer + 1) * 2 * OWN, :] = (
            (acc[...] / whole).astype(jnp.bfloat16).reshape(RANKS, 2 * OWN, HD)
        )
        rest = peak[...] * EXP_SCALE + jnp.log(whole) * math.log2(math.e)
        kept = side[...] if layer else jnp.zeros((QROWS, HD), jnp.float32)
        for i in range(3):
            term = rest.astype(jnp.bfloat16).astype(jnp.float32)
            rest = rest - term
            kept = jnp.where(lane == 3 * layer + i, term, kept)
        side[...] = kept

    def rank_copy(src, dst, s_sem, rr_sem, k):
        target = k - 1 + (k - 1 - z + RANKS) // RANKS
        return copy_of(
            src(target), dst(z), s_sem.at[target], rr_sem.at[z], rank_device(target)
        )

    def rank_arrived(src, dst, s_sem, rr_sem, k):
        other = (z + k) % RANKS
        copy_of(
            src(other), dst(other), s_sem.at[other], rr_sem.at[other], rank_device(other)
        ).wait_recv()

    def run_of(ref, layer):
        return lambda rank: ref.at[rank, 0:32] if layer == 0 else ref.at[rank, 32:80]

    attention = [
        (run_of(asend, layer), run_of(arecv, layer), as_sem.at[layer], ar_sem.at[layer])
        for layer in range(LAYERS)
    ]
    project = (lambda rank: psend.at[rank], lambda rank: precv.at[rank], ps_sem, pr_sem)

    def answered():
        answers = (RANKS - 1 - z) + (1 - xl)
        pl.when(answers > 0)(lambda: pl.semaphore_wait(token_sem, answers))

    def send_attention(layer):
        loop(1, RANKS, lambda k: rank_copy(*attention[layer], k).start())

    def send_project():
        loop(1, RANKS, lambda k: rank_copy(*project, k).start())

    load_k.wait()
    scores(0)
    loop(1, CHIPS, h_arrived)
    h_sib(c).start()
    load_v.wait()
    values(0)

    @pl.when(high_rank)
    def _():
        answered()
        send_attention(0)

    for layer in range(LAYERS):
        sib_send(0, layer)
    pl.when(low)(lambda: loop(0, 2, y2_step))
    h_sib(1 - c).wait_recv()

    rows8 = lax.broadcasted_iota(jnp.int32, (SLOTS, LAYERS * STEPS, HD), 1)
    product = []
    for layer in range(LAYERS):
        halves = [
            jnp.dot(
                hall[...].reshape(SLOTS * 16, 256), gat[me, layer, h * 256 : (h + 1) * 256, :],
                preferred_element_type=jnp.float32,
            ).reshape(SLOTS, 16, HD)
            for h in range(2)
        ]
        product.append(halves[0][:, :8] + halves[1][:, 8:])
    part[...] = jnp.where(rows8 < STEPS, product[0], product[1])

    def part_copy(k):
        target = (me + k) % SLOTS
        return copy_of(
            part.at[(target % 2) * CHIPS + target // 2], proj.at[me],
            part_sem.at[target], part_r_sem.at[me], (target, t),
        )

    def part_arrived(k):
        other = (me + k) % SLOTS
        copy_of(
            part.at[other], proj.at[other], part_sem.at[other], part_r_sem.at[other], to_sib
        ).wait_recv()

    loop(1, SLOTS, lambda k: part_copy(k).start())
    proj[me] = part[c * CHIPS + chip]

    scores(1)
    @pl.when(low)
    def _():
        loop(2, CHUNKS, y2_step)
        loop(0, 2, cross_step)

    pl.when(high_rank)(lambda: loop(0, 2, y2_step))
    values(1)
    notes = side[...].reshape(RANKS, 2 * OWN, HD)
    second = pltpu.roll(notes[:, OWN:].reshape(RANKS * OWN, HD), HD // 2, 1)
    lane3 = lax.broadcasted_iota(jnp.int32, (RANKS, OWN, HD), 2)
    notes = jnp.where(lane3 < HD // 2, notes[:, :OWN], second.reshape(RANKS, OWN, HD))
    asend[:, 4 * OWN :, :] = notes.astype(jnp.bfloat16)
    @pl.when(high_rank)
    def _():
        send_attention(1)
        loop(2, CHUNKS, y2_step)
        loop(0, 2, cross_step)


    def opposite_step(j):
        arrived(slot_of(xh, (y + 4 + 1 - 2 * (j % 2)) % 4, c), j)

    def far_steps():
        loop(2, CHUNKS, far_step)
        loop(0, CHUNKS, opposite_step)
        for layer in range(LAYERS):
            for i in range(4):
                sib_send(i + 1, layer)

    @pl.when(low)
    def _():
        loop(2, CHUNKS, cross_step)
        loop(0, 2, far_step)
        far_steps()
        answered()
        send_attention(0)
        send_attention(1)

    loop(1, SLOTS, part_arrived)
    for g in range(SLOTS):
        slot_all = jnp.broadcast_to(map_ref[g], (LAYERS * STEPS, HD))
        line = proj[0]
        for slot in range(1, SLOTS):
            line = jnp.where(slot_all == slot, proj[slot], line)
        psend[g // 2, (g % 2) * 8 : (g % 2) * 8 + 8, :] = line
    precv[z] = psend[z]
    arecv[z] = asend[z]

    send_project()

    @pl.when(high_rank)
    def _():
        loop(2, CHUNKS, cross_step)
        loop(0, 2, far_step)
        far_steps()

    load_bias.wait()
    load_inv.wait()
    turn_row = lax.broadcasted_iota(jnp.int32, (LAYERS * STEPS, HD), 0)
    turn_lane = lax.broadcasted_iota(jnp.int32, (LAYERS * STEPS, HD), 1)
    angle = (length + turn_row % STEPS).astype(jnp.float32) * inv_ref[...]
    cosine = jnp.cos(angle)
    sine = jnp.where(turn_lane < HD // 2, -1.0, 1.0) * jnp.sin(angle)
    head = t // 2
    bias = bias_ref[:, pl.ds(pl.multiple_of(head * 2 * HD, 2 * HD), 2 * HD)].astype(jnp.float32)

    def last_pieces(layer):
        for i, slot in ((5, x_up), (6, x_down), (7, x_far)):
            loop(2 * layer, 2 * layer + 2, lambda j, slot=slot: arrived(slot, j))
            sib_send(i, layer)

    last_pieces(0)
    pl.when(z < 3)(lambda: last_pieces(1))

    for layer in range(LAYERS):
        loop(1, RANKS, lambda k, layer=layer: rank_arrived(*attention[layer], k))
    lane32 = lax.broadcasted_iota(jnp.int32, (2 * OWN, HD), 1)
    sides = [arecv[p, 4 * OWN :, :].astype(jnp.float32) for p in range(RANKS)]
    notes = jnp.zeros((2 * OWN, HD), jnp.float32)
    for layer in range(LAYERS):
        logs = []
        for x in sides:
            firsts = (3 * layer, 3 * layer + HD // 2)
            columns = [sum(x[:, n + i : n + i + 1] for i in range(3)) for n in firsts]
            logs.append(jnp.concatenate(columns, axis=0))
        high = functools.reduce(jnp.maximum, logs)
        whole = jnp.zeros((2 * OWN, 1), jnp.float32)
        summed = jnp.zeros((2 * OWN, HD), jnp.float32)
        rows = slice(layer * 2 * OWN, (layer + 1) * 2 * OWN)
        for p in range(RANKS):
            factor = jnp.exp2(logs[p] - high)
            whole = whole + factor
            summed = summed + factor * arecv[p, rows, :].astype(jnp.float32)
        for o in range(2):
            pair_own[o, layer * OWN : (layer + 1) * OWN, :] = summed[o * OWN : (o + 1) * OWN]
        notes = jnp.where(lane32 == 2 * layer, high, notes)
        notes = jnp.where(lane32 == 2 * layer + 1, whole, notes)
    for o in range(2):
        pair_own[o, 2 * OWN : 3 * OWN, :] = notes[o * OWN : (o + 1) * OWN]

    def pair_copy(n, low_row, count):
        rows = pl.ds(low_row, count)
        return copy_of(
            pair_own.at[1 - xl, rows, :], pair_in.at[rows, :],
            pair_sem.at[n, 0], pair_sem.at[n, 1], to_pair,
        )

    pair = [pair_copy(0, 0, 3 * OWN), pair_copy(1, 3 * OWN, OWN)]
    pair[0].start()
    loop(1, RANKS, lambda k: rank_arrived(*project, k))
    projected = precv[0]
    for p in range(1, RANKS):
        projected = projected + precv[p]
    for o in range(2):
        pair_own[o, 3 * OWN :, :] = projected
    pair[1].start()
    pl.when(z >= 3)(lambda: last_pieces(1))
    pair[0].wait_recv()
    joined = []
    for layer in range(LAYERS):
        sums, highs, wholes = [], [], []
        for half in (pair_own.at[xl], pair_in):
            sums.append(half[layer * OWN : (layer + 1) * OWN, :])
            highs.append(half[2 * OWN : 3 * OWN, 2 * layer : 2 * layer + 1])
            wholes.append(half[2 * OWN : 3 * OWN, 2 * layer + 1 : 2 * layer + 2])
        high = jnp.maximum(*highs)
        factors = [jnp.exp2(h - high) for h in highs]
        whole = wholes[0] * factors[0] + wholes[1] * factors[1]
        summed = sums[0] * factors[0] + sums[1] * factors[1]
        joined.append((high, whole, summed))
    pair[1].wait_recv()
    projected = (pair_own[xl, 3 * OWN :, :] + pair_in[3 * OWN :, :]) * (ROWS * PEERS) ** -0.5

    def biased(kind):
        lines = [
            jnp.broadcast_to(bias[layer : layer + 1, kind * HD : (kind + 1) * HD], (8, HD))
            for layer in range(LAYERS)
        ]
        return projected[kind * 8 : kind * 8 + 8] + jnp.where(turn_row < STEPS, lines[0], lines[1])

    key = biased(0)
    key = (key * cosine + pltpu.roll(key, HD // 2, 1) * sine).astype(jnp.bfloat16)
    value = biased(1).astype(jnp.bfloat16)
    row = lax.broadcasted_iota(jnp.int32, (OWN, LAYERS * STEPS), 0)
    col = lax.broadcasted_iota(jnp.int32, (OWN, LAYERS * STEPS), 1)
    for layer in range(LAYERS):
        query = qp[layer, pl.ds(pl.multiple_of(t * OWN, OWN), OWN), :]
        s = lax.dot_general(
            query, key, (((1,), (1,)), ((), ())), preferred_element_type=jnp.float32
        )
        allowed = (col // STEPS == layer) & (col % STEPS <= row // STEPS)
        s = jnp.where(allowed, s * EXP_SCALE, NEG)
        high, whole, summed = joined[layer]
        top_all = jnp.maximum(high, jnp.max(s, axis=1, keepdims=True))
        e = jnp.exp2(s - top_all)
        factor = jnp.exp2(high - top_all)
        whole = whole * factor + jnp.sum(e, axis=1, keepdims=True)
        summed = summed * factor + jnp.dot(
            e.astype(jnp.bfloat16), value, preferred_element_type=jnp.float32
        )
        result = (summed / whole).astype(jnp.bfloat16)
        for step in range(STEPS):
            out_ref[layer, 0, step] = result[step * 4 : step * 4 + 4]

    for i, slot in enumerate([me] + others):
        for layer in range(LAYERS):
            sib_copy(i, flip(slot), layer).wait_recv()
            sib_copy(i, slot, layer).wait_send()

    def sent(j):
        for copy in own_copies(j) + cross_copies(j) + [y2_copy(j), far_copy(j)]:
            copy.wait_send()

    loop(0, CHUNKS, sent)
    loop(1, CHIPS, lambda k: h_copy(k).wait_send())
    h_sib(c).wait_send()
    loop(1, SLOTS, lambda k: part_copy(k).wait_send())
    for layer in range(LAYERS):
        loop(1, RANKS, lambda k, layer=layer: rank_copy(*attention[layer], k).wait_send())
    loop(1, RANKS, lambda k: rank_copy(*project, k).wait_send())
    for copy in pair:
        copy.wait_send()


def place_kernel(map_ref, gat, part, out_hbm, part_out, sem, part_sem):
    last = pltpu.make_async_copy(part, part_out, part_sem)
    last.start()
    copies = []
    for group in range(SLOTS):
        for layer in range(LAYERS):
            copy = pltpu.make_async_copy(
                gat.at[map_ref[group], layer],
                out_hbm.at[layer, :, pl.ds(group * HD, HD)],
                sem.at[group, layer],
            )
            copy.start()
            copies.append(copy)
    for copy in copies:
        copy.wait()
    last.wait()


def on_device(
    hidden, resident, delta_codes, scales, owner_map, key_value_bias, queries, key_cache,
    value_cache, lengths,
):
    inverse = (ROPE_BASE ** (-2.0 * np.arange(HD // 2) / HD)).astype(np.float32)
    inverse = jnp.asarray(np.concatenate([inverse, inverse])[None, :])
    smem = pl.BlockSpec(memory_space=pltpu.SMEM)
    vmem = pl.BlockSpec(memory_space=pltpu.VMEM)
    hbm = pl.BlockSpec(memory_space=pltpu.HBM)
    anywhere = pl.BlockSpec(memory_space=pl.ANY)
    dma = pltpu.SemaphoreType.DMA
    f32, bf16 = jnp.float32, jnp.bfloat16
    part_shape = (LAYERS, 1, STEPS, HEADS // PEERS, HD)
    arrays = (
        owner_map, lengths, hidden, resident, delta_codes,
        scales.reshape(LAYERS, ROWS), key_value_bias, inverse,
        queries.reshape(LAYERS, QROWS, HD),
        key_cache.reshape(LAYERS, COLS, HD), value_cache.reshape(LAYERS, COLS, HD),
    )
    gathered, part, chosen = pl.pallas_call(
        gather_kernel,
        out_shape=(
            pltpu.VMEM((SLOTS, LAYERS, ROWS, HD), bf16),
            jax.ShapeDtypeStruct(part_shape, bf16),
            pltpu.SMEM((SLOTS,), jnp.int32),
        ),
        in_specs=[hbm, smem] + [hbm] * 9,
        out_specs=(vmem, vmem, smem),
        scratch_shapes=[
            pltpu.SMEM((SLOTS,), jnp.int32),
            pltpu.VMEM((LAYERS, 1, STEPS, ROWS), bf16),
            pltpu.VMEM((LAYERS, ROWS, SLOTS * HD), bf16),
            pltpu.VMEM((LAYERS, ROWS, HD), bf16),
            pltpu.VMEM((LAYERS, ROWS), bf16),
            pltpu.VMEM((LAYERS, SLOTS * HD), bf16),
            pltpu.VMEM((1, HD), f32),
            pltpu.VMEM((LAYERS, QROWS, HD), bf16),
            pltpu.VMEM((LAYERS, COLS, HD), bf16),
            pltpu.VMEM((LAYERS, COLS, HD), bf16),
            pltpu.VMEM((2, CHIPS, 16, 256), bf16),
            pltpu.VMEM((LAYERS, QROWS, HD), bf16),
            pltpu.VMEM((QROWS, COLS), f32),
            pltpu.VMEM((QROWS, HD), f32),
            pltpu.VMEM((QROWS, HD), f32),
            pltpu.VMEM((QROWS, HD), f32),
            pltpu.VMEM((QROWS, HD), f32),
            pltpu.VMEM((QROWS, HD), f32),
            pltpu.VMEM((RANKS, 5 * OWN, HD), bf16),
            pltpu.VMEM((RANKS, 5 * OWN, HD), bf16),
            pltpu.VMEM((SLOTS, LAYERS * STEPS, HD), f32),
            pltpu.VMEM((SLOTS, LAYERS * STEPS, HD), f32),
            pltpu.VMEM((RANKS, 16, HD), f32),
            pltpu.VMEM((RANKS, 16, HD), f32),
            pltpu.VMEM((2, 4 * OWN, HD), f32),
            pltpu.VMEM((4 * OWN, HD), f32),
            dma((13,)),
            dma((SLOTS, CHUNKS)),
            dma((SLOTS, LAYERS)),
            dma((3, CHUNKS)),
            dma((CHUNKS,)),
            dma((2, CHUNKS)),
            dma((CHUNKS,)),
            dma((8, LAYERS)),
            dma((CHIPS + 1,)),
            dma((CHIPS,)),
            pltpu.SemaphoreType.REGULAR,
            dma((LAYERS, RANKS)),
            dma((LAYERS, RANKS)),
            dma((SLOTS,)),
            dma((SLOTS,)),
            dma((RANKS,)),
            dma((RANKS,)),
            dma((2, 2)),
        ],
        compiler_params=pltpu.CompilerParams(
            collective_id=0, has_side_effects=True, vmem_limit_bytes=40 * MIB
        ),
    )(*(a if a.size == 1 else pltpu.with_memory_space_constraint(a, pltpu.HBM) for a in arrays))
    return pl.pallas_call(
        place_kernel,
        out_shape=(
            jax.ShapeDtypeStruct((LAYERS, ROWS, SLOTS * HD), bf16),
            jax.ShapeDtypeStruct(part_shape, bf16),
        ),
        in_specs=[smem, vmem, vmem],
        out_specs=(anywhere, anywhere),
        scratch_shapes=[dma((SLOTS, LAYERS)), dma(())],
        compiler_params=pltpu.CompilerParams(vmem_limit_bytes=16 * MIB),
    )(chosen, gathered, part)


def solution(mesh):
    in_specs = (
        P(None, "replica", None, "tensor"),
        P(None, "tensor", None),
        P(None, "tensor", "replica"),
        P(None, "tensor", "replica"),
        P(),
        P(),
        P(None, "replica", None, None, None),
        P(None, "replica", "tensor", None, None),
        P(None, "replica", "tensor", None, None),
        P("replica"),
    )
    out_specs = (P(None, "tensor", None), P(None, "replica", None, "tensor", None))
    return jax.shard_map(
        on_device, mesh=mesh, in_specs=in_specs, out_specs=out_specs, check_vma=False
    )
```

```python
import functools
import math

import jax
import jax.numpy as jnp
import numpy as np
from jax import lax
from jax.experimental import pallas as pl
from jax.experimental.pallas import tpu as pltpu
from jax.sharding import PartitionSpec as P

MESH = pl.DeviceIdType.MESH
ROPE_BASE = 1000000.0
MIB = 1 << 20
NEG = -1e30

LAYERS = 2
STEPS = 4
ROWS = 512
HD = 128
SLOTS = 16
PEERS = 16
RANKS = 8
STRIPE = 64
HEADS = 64
KVH = 8
QROWS = STEPS * HEADS
OWN = QROWS // PEERS
SPOTS = 512
COLS = SPOTS * KVH
WIDE = 1024
CHIPS = 8
CHUNKS = 4
HALF = ROWS * LAYERS // CHUNKS
EXP_SCALE = HD**-0.5 * math.log2(math.e)


def place():
    replica = lax.axis_index("replica")
    return replica // 8, (replica // 2) % 4, replica % 2, lax.axis_index("tensor")


def slot_of(xh, y, c):
    return (xh * 4 + y) * 2 + c


def gather_kernel(
    map_hbm, len_ref, hid_hbm, res_hbm, code_hbm, scale_hbm, bias_hbm, inv_hbm, q_hbm, k_hbm, v_hbm,
    gat, out_ref, map_out,
    map_ref, hid_ref, res, code_ref, scale_ref, bias_ref, inv_ref, q_ref, kbuf, vbuf,
    hall, qp, sbuf, top, peak, total, acc, side, asend, arecv, part, proj, psend, precv, pair_own, pair_in,
    load_sem, r_sem, sib_r_sem, own_sem, y2_sem, cross_sem, far_sem, sib_sem,
    h_r_sem, h_sem, token_sem, as_sem, ar_sem, part_sem, part_r_sem, ps_sem, pr_sem, pair_sem,
):
    xh, y, c, t = place()
    me = slot_of(xh, y, c)

    pairs = [
        (map_hbm, map_ref), (hid_hbm, hid_ref), (scale_hbm, scale_ref), (code_hbm, code_ref),
    ]
    for j in range(CHUNKS):
        rows = pl.ds((j % 2) * HALF, HALF)
        pairs.append((res_hbm.at[j // 2, rows, :], res.at[j // 2, rows, :]))
    pairs += [
        (q_hbm, q_ref), (k_hbm, kbuf), (v_hbm, vbuf), (bias_hbm, bias_ref), (inv_hbm, inv_ref),
    ]
    loads = [pltpu.make_async_copy(a, b, load_sem.at[i]) for i, (a, b) in enumerate(pairs)]
    load_map, load_hid, load_scale, load_code = loads[:4]
    load_res, (load_q, load_k, load_v, load_bias, load_inv) = loads[4:8], loads[8:]
    for load in loads[:8]:
        load.start()

    def loop(low, high, body):
        def step(j, carry):
            body(j)
            return carry

        lax.fori_loop(low, high, step, 0)

    def device(x2, y2, c2):
        return (slot_of(x2, y2, c2), t)

    y_up, y_down, y_far = (y + 1) % 4, (y + 3) % 4, (y + 2) % 4
    to_up, to_down = device(xh, y_up, c), device(xh, y_down, c)
    to_x, to_sib = device(1 - xh, y, c), device(xh, y, 1 - c)

    barrier = pltpu.get_barrier_semaphore()
    chip = xh * 4 + y
    pl.semaphore_signal(barrier, inc=1, device_id=to_sib, device_id_type=MESH)

    def chip_device(k):
        return (((chip + k) % CHIPS) * 2 + c, t)

    def greet_chip(k):
        pl.semaphore_signal(barrier, inc=1, device_id=chip_device(k), device_id_type=MESH)

    loop(1, CHIPS, greet_chip)

    z, xl = t // 2, t % 2
    low, high_rank = z < RANKS // 2, z >= RANKS // 2

    def rank_device(k):
        return (me, k * 2 + xl)

    to_pair = (me, z * 2 + 1 - xl)

    def greet(k):
        pl.semaphore_signal(barrier, inc=1, device_id=rank_device(k), device_id_type=MESH)

    loop(z + 1, RANKS, greet)

    @pl.when(xl == 0)
    def _():
        pl.semaphore_signal(barrier, inc=1, device_id=to_pair, device_id_type=MESH)

    load_map.wait()
    group = jnp.int32(0)
    for g in range(SLOTS):
        group = group + jnp.where(map_ref[g] == me, g, 0)
        map_out[g] = map_ref[g]
    group_all = jnp.broadcast_to(group.astype(jnp.float32), (HD, HD)).astype(jnp.bfloat16)

    def own_block(j):
        load_res[j].wait()
        layer = j // 2
        for p in range(HALF // HD):
            rows = pl.ds((j % 2) * HALF + p * HD, HD)
            line = scale_ref[pl.ds(layer, 1), rows].astype(jnp.float32)
            column = jnp.transpose(jnp.broadcast_to(line, (HD, HD)))
            code = code_ref[layer, rows, :].astype(jnp.float32)
            base = res[layer, rows, :HD]
            for g in range(1, SLOTS):
                base = jnp.where(group_all == g, res[layer, rows, g * HD : (g + 1) * HD], base)
            base = base.astype(jnp.float32)
            gat[me, layer, rows, :] = (base + code * column).astype(jnp.bfloat16)

    load_hid.wait()
    halves = [
        hid_ref[layer, 0, :, h * 256 : (h + 1) * 256].astype(jnp.float32)
        for h in range(2)
        for layer in range(LAYERS)
    ]
    hall[c, chip] = jnp.concatenate(halves, axis=0).astype(jnp.bfloat16)

    pl.semaphore_wait(barrier, CHIPS + z + xl)

    def copy_of(src, dst, s_sem, rr_sem, target):
        return pltpu.make_async_remote_copy(
            src_ref=src, dst_ref=dst, send_sem=s_sem, recv_sem=rr_sem,
            device_id=target, device_id_type=MESH,
        )

    s_up, s_down = slot_of(xh, y_up, c), slot_of(xh, y_down, c)
    s_far, s_x = slot_of(xh, y_far, c), slot_of(1 - xh, y, c)
    x_up, x_down = slot_of(1 - xh, y_up, c), slot_of(1 - xh, y_down, c)
    x_far = slot_of(1 - xh, y_far, c)
    others = [s_up, s_down, s_x, s_far, x_up, x_down, x_far]

    def flip(slot):
        return slot + 1 - 2 * c

    def h_copy(k):
        return copy_of(
            hall.at[c, chip], hall.at[c, chip], h_sem.at[k], h_r_sem.at[chip], chip_device(k)
        )

    def h_arrived(k):
        other = (chip + k) % CHIPS
        copy_of(
            hall.at[c, other], hall.at[c, other], h_sem.at[k], h_r_sem.at[other], to_sib
        ).wait_recv()

    def h_sib(core):
        return copy_of(hall.at[core], hall.at[core], h_sem.at[0], h_r_sem.at[CHIPS], to_sib)

    def rows_of(slot, j, count):
        return gat.at[slot, j // 2, pl.ds(pl.multiple_of((j % 2) * HALF, HALF), HALF * count), :]

    def send(slot, j, sem, target):
        ref = rows_of(slot, j, 1)
        return copy_of(ref, ref, sem, r_sem.at[slot, j], target)

    def arrived(slot, j):
        send(slot, j, r_sem.at[slot, j], to_sib).wait_recv()

    def sib_copy(i, slot, layer):
        ref = gat.at[slot, layer]
        return copy_of(ref, ref, sib_sem.at[i, layer], sib_r_sem.at[slot, layer], to_sib)

    def sib_send(i, layer):
        sib_copy(i, others[i - 1] if i else me, layer).start()

    def own_copies(j):
        return [
            send(me, j, own_sem.at[0, j], to_up),
            send(me, j, own_sem.at[1, j], to_down),
            send(me, j, own_sem.at[2, j], to_x),
        ]

    def onward(j):
        up = 1 - 2 * (j % 2)
        return slot_of(xh, (y + 4 - up) % 4, c), device(xh, (y + 4 + up) % 4, c)

    def y2_copy(j):
        slot, target = onward(j)
        return send(slot, j, y2_sem.at[j], target)

    def cross_copies(j):
        return [send(s_x, j, cross_sem.at[0, j], to_up), send(s_x, j, cross_sem.at[1, j], to_down)]

    def far_copy(j):
        return send(s_far, j, far_sem.at[j], to_x)

    def y2_step(j):
        slot, _ = onward(j)
        arrived(slot, j)
        y2_copy(j).start()

    def cross_step(j):
        arrived(s_x, j)
        for copy in cross_copies(j):
            copy.start()

    def far_step(j):
        arrived(s_far, j)
        far_copy(j).start()

    loop(1, CHIPS, lambda k: h_copy(k).start())

    def own_step(j):
        for copy in own_copies(j):
            copy.start()

    load_scale.wait()
    load_code.wait()
    for j in range(CHUNKS):
        own_block(j)
        own_step(j)
        if j == 0:
            for load in loads[8:]:
                load.start()

    def answer(k):
        pl.semaphore_signal(token_sem, inc=1, device_id=rank_device(k), device_id_type=MESH)

    loop(0, z, answer)

    @pl.when(xl == 1)
    def _():
        pl.semaphore_signal(token_sem, inc=1, device_id=to_pair, device_id_type=MESH)

    load_q.wait()
    row = lax.broadcasted_iota(jnp.int32, (QROWS, QROWS), 0)
    col = lax.broadcasted_iota(jnp.int32, (QROWS, QROWS), 1)
    source = ((row // STEPS) % STEPS) * HEADS + (row // OWN) * STEPS + row % STEPS
    pick = jnp.where(col == source, 1.0, 0.0).astype(jnp.bfloat16)
    for layer in range(LAYERS):
        qp[layer] = jnp.dot(pick, q_ref[layer], preferred_element_type=jnp.float32).astype(
            jnp.bfloat16
        )
    length = len_ref[0]
    limit = (length - t * SPOTS) * KVH
    lanes = lax.broadcasted_iota(jnp.int32, (1, WIDE), 1)
    lane = lax.broadcasted_iota(jnp.int32, (QROWS, HD), 1)
    valid = lane % KVH == lax.broadcasted_iota(jnp.int32, (QROWS, HD), 0) // (QROWS // KVH)

    def scores(layer):
        top[...] = jnp.full((QROWS, HD), NEG, jnp.float32)
        for n in range(COLS // WIDE):
            first = n * WIDE
            s = lax.dot_general(
                qp[layer], kbuf[layer, first : first + WIDE, :], (((1,), (1,)), ((), ())),
                preferred_element_type=jnp.float32,
            )
            s = s + jnp.where(lanes + first < limit, 0.0, NEG)
            sbuf[:, first : first + WIDE] = s
            high = top[...]
            for i in range(WIDE // HD):
                high = jnp.maximum(high, s[:, i * HD : (i + 1) * HD])
            top[...] = high
        high = jnp.max(jnp.where(valid, top[...], NEG), axis=1, keepdims=True)
        peak[...] = jnp.broadcast_to(high, (QROWS, HD))
        top[...] = jnp.where(valid, high, -NEG)

    def values(layer):
        total[...] = jnp.zeros((QROWS, HD), jnp.float32)
        acc[...] = jnp.zeros((QROWS, HD), jnp.float32)
        for n in range(COLS // WIDE):
            first = n * WIDE
            high = top[...]
            added = total[...]
            pieces = []
            for i in range(WIDE // HD):
                e = jnp.exp2((sbuf[:, first + i * HD : first + (i + 1) * HD] - high) * EXP_SCALE)
                added = added + e
                pieces.append(e.astype(jnp.bfloat16))
            total[...] = added
            acc[...] += jnp.dot(
                jnp.concatenate(pieces, axis=1), vbuf[layer, first : first + WIDE, :],
                preferred_element_type=jnp.float32,
            )
        whole = jnp.broadcast_to(jnp.sum(total[...], axis=1, keepdims=True), (QROWS, HD))
        asend[:, layer * 2 * OWN : (layer + 1) * 2 * OWN, :] = (
            (acc[...] / whole).astype(jnp.bfloat16).reshape(RANKS, 2 * OWN, HD)
        )
        rest = peak[...] * EXP_SCALE + jnp.log(whole) * math.log2(math.e)
        kept = side[...] if layer else jnp.zeros((QROWS, HD), jnp.float32)
        for i in range(3):
            term = rest.astype(jnp.bfloat16).astype(jnp.float32)
            rest = rest - term
            kept = jnp.where(lane == 3 * layer + i, term, kept)
        side[...] = kept

    def rank_copy(src, dst, s_sem, rr_sem, k):
        target = k - 1 + (k - 1 - z + RANKS) // RANKS
        return copy_of(
            src(target), dst(z), s_sem.at[target], rr_sem.at[z], rank_device(target)
        )

    def rank_arrived(src, dst, s_sem, rr_sem, k):
        other = (z + k) % RANKS
        copy_of(
            src(other), dst(other), s_sem.at[other], rr_sem.at[other], rank_device(other)
        ).wait_recv()

    def run_of(ref, layer):
        return lambda rank: ref.at[rank, 0:32] if layer == 0 else ref.at[rank, 32:80]

    attention = [
        (run_of(asend, layer), run_of(arecv, layer), as_sem.at[layer], ar_sem.at[layer])
        for layer in range(LAYERS)
    ]
    project = (lambda rank: psend.at[rank], lambda rank: precv.at[rank], ps_sem, pr_sem)

    def answered():
        answers = (RANKS - 1 - z) + (1 - xl)
        pl.when(answers > 0)(lambda: pl.semaphore_wait(token_sem, answers))

    def send_attention(layer):
        loop(1, RANKS, lambda k: rank_copy(*attention[layer], k).start())

    def send_project():
        loop(1, RANKS, lambda k: rank_copy(*project, k).start())

    load_k.wait()
    scores(0)
    loop(1, CHIPS, h_arrived)
    h_sib(c).start()
    load_v.wait()
    values(0)

    @pl.when(high_rank)
    def _():
        answered()
        send_attention(0)

    for layer in range(LAYERS):
        sib_send(0, layer)
    pl.when(low)(lambda: loop(0, 2, y2_step))
    h_sib(1 - c).wait_recv()

    rows8 = lax.broadcasted_iota(jnp.int32, (SLOTS, LAYERS * STEPS, HD), 1)
    product = []
    for layer in range(LAYERS):
        halves = [
            jnp.dot(
                hall[...].reshape(SLOTS * 16, 256), gat[me, layer, h * 256 : (h + 1) * 256, :],
                preferred_element_type=jnp.float32,
            ).reshape(SLOTS, 16, HD)
            for h in range(2)
        ]
        product.append(halves[0][:, :8] + halves[1][:, 8:])
    part[...] = jnp.where(rows8 < STEPS, product[0], product[1])

    def part_copy(k):
        target = (me + k) % SLOTS
        return copy_of(
            part.at[(target % 2) * CHIPS + target // 2], proj.at[me],
            part_sem.at[target], part_r_sem.at[me], (target, t),
        )

    def part_arrived(k):
        other = (me + k) % SLOTS
        copy_of(
            part.at[other], proj.at[other], part_sem.at[other], part_r_sem.at[other], to_sib
        ).wait_recv()

    loop(1, SLOTS, lambda k: part_copy(k).start())
    proj[me] = part[c * CHIPS + chip]

    scores(1)
    @pl.when(low)
    def _():
        loop(2, CHUNKS, y2_step)
        loop(0, 2, cross_step)

    pl.when(high_rank)(lambda: loop(0, 2, y2_step))
    values(1)
    notes = side[...].reshape(RANKS, 2 * OWN, HD)
    second = pltpu.roll(notes[:, OWN:].reshape(RANKS * OWN, HD), HD // 2, 1)
    lane3 = lax.broadcasted_iota(jnp.int32, (RANKS, OWN, HD), 2)
    notes = jnp.where(lane3 < HD // 2, notes[:, :OWN], second.reshape(RANKS, OWN, HD))
    asend[:, 4 * OWN :, :] = notes.astype(jnp.bfloat16)
    @pl.when(high_rank)
    def _():
        send_attention(1)
        loop(2, CHUNKS, y2_step)
        loop(0, 2, cross_step)


    def opposite_step(j):
        arrived(slot_of(xh, (y + 4 + 1 - 2 * (j % 2)) % 4, c), j)

    def far_steps():
        loop(2, CHUNKS, far_step)
        loop(0, CHUNKS, opposite_step)
        for layer in range(LAYERS):
            for i in range(4):
                sib_send(i + 1, layer)

    @pl.when(low)
    def _():
        loop(2, CHUNKS, cross_step)
        loop(0, 2, far_step)
        far_steps()
        answered()
        send_attention(0)
        send_attention(1)

    loop(1, SLOTS, part_arrived)
    for g in range(SLOTS):
        slot_all = jnp.broadcast_to(map_ref[g], (LAYERS * STEPS, HD))
        line = proj[0]
        for slot in range(1, SLOTS):
            line = jnp.where(slot_all == slot, proj[slot], line)
        psend[g // 2, (g % 2) * 8 : (g % 2) * 8 + 8, :] = line
    precv[z] = psend[z]
    arecv[z] = asend[z]

    send_project()

    @pl.when(high_rank)
    def _():
        loop(2, CHUNKS, cross_step)
        loop(0, 2, far_step)
        far_steps()

    load_bias.wait()
    load_inv.wait()
    turn_row = lax.broadcasted_iota(jnp.int32, (LAYERS * STEPS, HD), 0)
    turn_lane = lax.broadcasted_iota(jnp.int32, (LAYERS * STEPS, HD), 1)
    angle = (length + turn_row % STEPS).astype(jnp.float32) * inv_ref[...]
    cosine = jnp.cos(angle)
    sine = jnp.where(turn_lane < HD // 2, -1.0, 1.0) * jnp.sin(angle)
    head = t // 2
    bias = bias_ref[:, pl.ds(pl.multiple_of(head * 2 * HD, 2 * HD), 2 * HD)].astype(jnp.float32)

    def last_pieces(layer):
        for i, slot in ((5, x_up), (6, x_down), (7, x_far)):
            loop(2 * layer, 2 * layer + 2, lambda j, slot=slot: arrived(slot, j))
            sib_send(i, layer)

    last_pieces(0)
    pl.when(z < 3)(lambda: last_pieces(1))

    for layer in range(LAYERS):
        loop(1, RANKS, lambda k, layer=layer: rank_arrived(*attention[layer], k))
    lane32 = lax.broadcasted_iota(jnp.int32, (2 * OWN, HD), 1)
    sides = [arecv[p, 4 * OWN :, :].astype(jnp.float32) for p in range(RANKS)]
    notes = jnp.zeros((2 * OWN, HD), jnp.float32)
    for layer in range(LAYERS):
        logs = []
        for x in sides:
            firsts = (3 * layer, 3 * layer + HD // 2)
            columns = [sum(x[:, n + i : n + i + 1] for i in range(3)) for n in firsts]
            logs.append(jnp.concatenate(columns, axis=0))
        high = functools.reduce(jnp.maximum, logs)
        whole = jnp.zeros((2 * OWN, 1), jnp.float32)
        summed = jnp.zeros((2 * OWN, HD), jnp.float32)
        rows = slice(layer * 2 * OWN, (layer + 1) * 2 * OWN)
        for p in range(RANKS):
            factor = jnp.exp2(logs[p] - high)
            whole = whole + factor
            summed = summed + factor * arecv[p, rows, :].astype(jnp.float32)
        for o in range(2):
            pair_own[o, layer * OWN : (layer + 1) * OWN, :] = summed[o * OWN : (o + 1) * OWN]
        notes = jnp.where(lane32 == 2 * layer, high, notes)
        notes = jnp.where(lane32 == 2 * layer + 1, whole, notes)
    for o in range(2):
        pair_own[o, 2 * OWN : 3 * OWN, :] = notes[o * OWN : (o + 1) * OWN]

    def pair_copy(n, low_row, count):
        rows = pl.ds(low_row, count)
        return copy_of(
            pair_own.at[1 - xl, rows, :], pair_in.at[rows, :],
            pair_sem.at[n, 0], pair_sem.at[n, 1], to_pair,
        )

    pair = [pair_copy(0, 0, 3 * OWN), pair_copy(1, 3 * OWN, OWN)]
    pair[0].start()
    loop(1, RANKS, lambda k: rank_arrived(*project, k))
    projected = precv[0]
    for p in range(1, RANKS):
        projected = projected + precv[p]
    for o in range(2):
        pair_own[o, 3 * OWN :, :] = projected
    pair[1].start()
    pl.when(z >= 3)(lambda: last_pieces(1))
    pair[0].wait_recv()
    joined = []
    for layer in range(LAYERS):
        sums, highs, wholes = [], [], []
        for half in (pair_own.at[xl], pair_in):
            sums.append(half[layer * OWN : (layer + 1) * OWN, :])
            highs.append(half[2 * OWN : 3 * OWN, 2 * layer : 2 * layer + 1])
            wholes.append(half[2 * OWN : 3 * OWN, 2 * layer + 1 : 2 * layer + 2])
        high = jnp.maximum(*highs)
        factors = [jnp.exp2(h - high) for h in highs]
        whole = wholes[0] * factors[0] + wholes[1] * factors[1]
        summed = sums[0] * factors[0] + sums[1] * factors[1]
        joined.append((high, whole, summed))
    pair[1].wait_recv()
    projected = (pair_own[xl, 3 * OWN :, :] + pair_in[3 * OWN :, :]) * (ROWS * PEERS) ** -0.5

    def biased(kind):
        lines = [
            jnp.broadcast_to(bias[layer : layer + 1, kind * HD : (kind + 1) * HD], (8, HD))
            for layer in range(LAYERS)
        ]
        return projected[kind * 8 : kind * 8 + 8] + jnp.where(turn_row < STEPS, lines[0], lines[1])

    key = biased(0)
    key = (key * cosine + pltpu.roll(key, HD // 2, 1) * sine).astype(jnp.bfloat16)
    value = biased(1).astype(jnp.bfloat16)
    row = lax.broadcasted_iota(jnp.int32, (OWN, LAYERS * STEPS), 0)
    col = lax.broadcasted_iota(jnp.int32, (OWN, LAYERS * STEPS), 1)
    for layer in range(LAYERS):
        query = qp[layer, pl.ds(pl.multiple_of(t * OWN, OWN), OWN), :]
        s = lax.dot_general(
            query, key, (((1,), (1,)), ((), ())), preferred_element_type=jnp.float32
        )
        allowed = (col // STEPS == layer) & (col % STEPS <= row // STEPS)
        s = jnp.where(allowed, s * EXP_SCALE, NEG)
        high, whole, summed = joined[layer]
        top_all = jnp.maximum(high, jnp.max(s, axis=1, keepdims=True))
        e = jnp.exp2(s - top_all)
        factor = jnp.exp2(high - top_all)
        whole = whole * factor + jnp.sum(e, axis=1, keepdims=True)
        summed = summed * factor + jnp.dot(
            e.astype(jnp.bfloat16), value, preferred_element_type=jnp.float32
        )
        result = (summed / whole).astype(jnp.bfloat16)
        for step in range(STEPS):
            out_ref[layer, 0, step] = result[step * 4 : step * 4 + 4]

    for i, slot in enumerate([me] + others):
        for layer in range(LAYERS):
            sib_copy(i, flip(slot), layer).wait_recv()
            sib_copy(i, slot, layer).wait_send()

    def sent(j):
        for copy in own_copies(j) + cross_copies(j) + [y2_copy(j), far_copy(j)]:
            copy.wait_send()

    loop(0, CHUNKS, sent)
    loop(1, CHIPS, lambda k: h_copy(k).wait_send())
    h_sib(c).wait_send()
    loop(1, SLOTS, lambda k: part_copy(k).wait_send())
    for layer in range(LAYERS):
        loop(1, RANKS, lambda k, layer=layer: rank_copy(*attention[layer], k).wait_send())
    loop(1, RANKS, lambda k: rank_copy(*project, k).wait_send())
    for copy in pair:
        copy.wait_send()


def place_kernel(map_ref, gat, part, out_hbm, part_out, rows_buf, sem, part_sem):
    last = pltpu.make_async_copy(part, part_out, part_sem)
    last.start()
    slots = [map_ref[group] for group in range(SLOTS)]
    copies = []
    for layer in range(LAYERS):
        for n in range(ROWS // STRIPE):
            rows = slice(n * STRIPE, (n + 1) * STRIPE)
            for group in range(SLOTS):
                rows_buf[layer, rows, group * HD : (group + 1) * HD] = gat[slots[group], layer, rows]
            copy = pltpu.make_async_copy(
                rows_buf.at[layer, rows, :], out_hbm.at[layer, rows, :], sem.at[layer, n]
            )
            copy.start()
            copies.append(copy)
    for copy in copies:
        copy.wait()
    last.wait()


def on_device(
    hidden, resident, delta_codes, scales, owner_map, key_value_bias, queries, key_cache,
    value_cache, lengths,
):
    inverse = (ROPE_BASE ** (-2.0 * np.arange(HD // 2) / HD)).astype(np.float32)
    inverse = jnp.asarray(np.concatenate([inverse, inverse])[None, :])
    smem = pl.BlockSpec(memory_space=pltpu.SMEM)
    vmem = pl.BlockSpec(memory_space=pltpu.VMEM)
    hbm = pl.BlockSpec(memory_space=pltpu.HBM)
    anywhere = pl.BlockSpec(memory_space=pl.ANY)
    dma = pltpu.SemaphoreType.DMA
    f32, bf16 = jnp.float32, jnp.bfloat16
    part_shape = (LAYERS, 1, STEPS, HEADS // PEERS, HD)
    arrays = (
        owner_map, lengths, hidden, resident, delta_codes,
        scales.reshape(LAYERS, ROWS), key_value_bias, inverse,
        queries.reshape(LAYERS, QROWS, HD),
        key_cache.reshape(LAYERS, COLS, HD), value_cache.reshape(LAYERS, COLS, HD),
    )
    gathered, part, chosen = pl.pallas_call(
        gather_kernel,
        out_shape=(
            pltpu.VMEM((SLOTS, LAYERS, ROWS, HD), bf16),
            jax.ShapeDtypeStruct(part_shape, bf16),
            pltpu.SMEM((SLOTS,), jnp.int32),
        ),
        in_specs=[hbm, smem] + [hbm] * 9,
        out_specs=(vmem, vmem, smem),
        scratch_shapes=[
            pltpu.SMEM((SLOTS,), jnp.int32),
            pltpu.VMEM((LAYERS, 1, STEPS, ROWS), bf16),
            pltpu.VMEM((LAYERS, ROWS, SLOTS * HD), bf16),
            pltpu.VMEM((LAYERS, ROWS, HD), bf16),
            pltpu.VMEM((LAYERS, ROWS), bf16),
            pltpu.VMEM((LAYERS, SLOTS * HD), bf16),
            pltpu.VMEM((1, HD), f32),
            pltpu.VMEM((LAYERS, QROWS, HD), bf16),
            pltpu.VMEM((LAYERS, COLS, HD), bf16),
            pltpu.VMEM((LAYERS, COLS, HD), bf16),
            pltpu.VMEM((2, CHIPS, 16, 256), bf16),
            pltpu.VMEM((LAYERS, QROWS, HD), bf16),
            pltpu.VMEM((QROWS, COLS), f32),
            pltpu.VMEM((QROWS, HD), f32),
            pltpu.VMEM((QROWS, HD), f32),
            pltpu.VMEM((QROWS, HD), f32),
            pltpu.VMEM((QROWS, HD), f32),
            pltpu.VMEM((QROWS, HD), f32),
            pltpu.VMEM((RANKS, 5 * OWN, HD), bf16),
            pltpu.VMEM((RANKS, 5 * OWN, HD), bf16),
            pltpu.VMEM((SLOTS, LAYERS * STEPS, HD), f32),
            pltpu.VMEM((SLOTS, LAYERS * STEPS, HD), f32),
            pltpu.VMEM((RANKS, 16, HD), f32),
            pltpu.VMEM((RANKS, 16, HD), f32),
            pltpu.VMEM((2, 4 * OWN, HD), f32),
            pltpu.VMEM((4 * OWN, HD), f32),
            dma((13,)),
            dma((SLOTS, CHUNKS)),
            dma((SLOTS, LAYERS)),
            dma((3, CHUNKS)),
            dma((CHUNKS,)),
            dma((2, CHUNKS)),
            dma((CHUNKS,)),
            dma((8, LAYERS)),
            dma((CHIPS + 1,)),
            dma((CHIPS,)),
            pltpu.SemaphoreType.REGULAR,
            dma((LAYERS, RANKS)),
            dma((LAYERS, RANKS)),
            dma((SLOTS,)),
            dma((SLOTS,)),
            dma((RANKS,)),
            dma((RANKS,)),
            dma((2, 2)),
        ],
        compiler_params=pltpu.CompilerParams(
            collective_id=0, has_side_effects=True, vmem_limit_bytes=40 * MIB
        ),
    )(*(a if a.size == 1 else pltpu.with_memory_space_constraint(a, pltpu.HBM) for a in arrays))
    return pl.pallas_call(
        place_kernel,
        out_shape=(
            jax.ShapeDtypeStruct((LAYERS, ROWS, SLOTS * HD), bf16),
            jax.ShapeDtypeStruct(part_shape, bf16),
        ),
        in_specs=[smem, vmem, vmem],
        out_specs=(anywhere, anywhere),
        scratch_shapes=[
            pltpu.VMEM((LAYERS, ROWS, SLOTS * HD), bf16),
            dma((LAYERS, ROWS // STRIPE)),
            dma(()),
        ],
        compiler_params=pltpu.CompilerParams(vmem_limit_bytes=16 * MIB),
    )(chosen, gathered, part)


def solution(mesh):
    in_specs = (
        P(None, "replica", None, "tensor"),
        P(None, "tensor", None),
        P(None, "tensor", "replica"),
        P(None, "tensor", "replica"),
        P(),
        P(),
        P(None, "replica", None, None, None),
        P(None, "replica", "tensor", None, None),
        P(None, "replica", "tensor", None, None),
        P("replica"),
    )
    out_specs = (P(None, "tensor", None), P(None, "replica", None, "tensor", None))
    return jax.shard_map(
        on_device, mesh=mesh, in_specs=in_specs, out_specs=out_specs, check_vma=False
    )
```
